32 devices in a mesh: group: 8 (over y, x, core), expert: 4 (over z).
Axes of the slice: x: 2, y: 2, z: 4, core: 2. Of those that a mesh axis runs over, the one named last changes fastest.
Arguments:
- tokens_in: bfloat16 [4096, 2048], P(('group', 'expert')), may hold values from -6 to 6
- out_grad: bfloat16 [4096, 2048], P(('group', 'expert')), may hold values from -3 to 3
- expert_ids: int32 [4096, 8], P(('group', 'expert')), may hold values from 0 to 31, as said below
- gate_weights: float32 [4096, 8], P(('group', 'expert')), may hold values from 0.05 to 1
- w_gate: bfloat16 [32, 2048, 768], P(('group', 'expert')), may hold values from -0.125 to 0.125
- w_up: bfloat16 [32, 2048, 768], P(('group', 'expert')), may hold values from -0.125 to 0.125
- w_down: bfloat16 [32, 768, 2048], P(('group', 'expert')), may hold values from -0.21875 to 0.21875
Outputs:
- grad_in: bfloat16 [4096, 2048], P(('group', 'expert'))
- grad_gate: bfloat16 [32, 2048, 768], P(('group', 'expert'))
- grad_up: bfloat16 [32, 2048, 768], P(('group', 'expert'))
- grad_down: bfloat16 [32, 768, 2048], P(('group', 'expert'))
The draws below stay inside these ranges and needn't reach their ends.
Inputs may be any that keep to these rules, and one draw needn't show every extreme that they name: `expert_ids`: each row names 8 different experts. Among the 128 tokens of one device no expert is named more than 64 times, and some expert is named exactly 64 times by the tokens of some device. The tokens of one device name the experts of each group (experts g * 4 to g * 4 + 3) exactly 128 times. Over all 4096 tokens every expert is named exactly 128 * 8 times.
All inputs are finite; a program needn't handle non-finite values.
Results may differ from the reference program's by a relative error of at most 0.0065.
Values may be sent and summed in bfloat16 or wider, within the bound.
No kernel may reach another device: no remote copies, remote signals or barrier semaphores. Data moves between devices by JAX's collectives and lax.ppermute only.
A program may use at most 128 MiB of HBM per device.

```python
import math
import jax
import jax.numpy as jnp
from jax import lax

D = 2048
FF = 768
TOP = 8
TOK_DEV = 128
EXPERTS = 32
TOKENS = 4096
CAP = 64
N_GROUP = 8
N_EXPERT = 4


def base_counts(key, half):
    rough = jax.random.randint(key, (N_GROUP, N_EXPERT // 2), 0, half + 1).at[0, 0].set(half)
    return jnp.concatenate([rough, half - rough], axis=1).astype(jnp.int32)


def spread_counts(base, order):
    group_shift = order // N_EXPERT
    owner_shift = order % N_EXPERT
    group_cols = jnp.arange(N_GROUP, dtype=jnp.int32)
    owner_cols = jnp.arange(N_EXPERT, dtype=jnp.int32)
    group_pick = (group_cols[None, :] + group_shift[:, None]) % N_GROUP
    owner_pick = (owner_cols[None, :] + owner_shift[:, None]) % N_EXPERT
    return base[group_pick[:, :, None], owner_pick[:, None, :]].reshape(EXPERTS, EXPERTS)


def draw_expert_ids(key, part):
    half = CAP // 2
    keys = jax.random.split(jax.random.fold_in(key, 7), 5)
    first_base = base_counts(keys[0], half)
    second_base = base_counts(keys[1], half)
    order_one = jax.random.permutation(keys[2], EXPERTS).astype(jnp.int32)
    mapping = jnp.concatenate([jnp.zeros((1,), jnp.int32), 1 + jax.random.permutation(keys[3], EXPERTS - 1).astype(jnp.int32)])
    order_two = order_one[mapping]
    block_counts = spread_counts(first_base, order_one) + spread_counts(second_base, order_two)
    block_ends = jnp.cumsum(block_counts, axis=1)
    occurrence = jnp.arange(TOK_DEV * TOP, dtype=jnp.int32)
    expert_of = jax.vmap(lambda ends_row: jnp.searchsorted(ends_row, occurrence, side='right'))(block_ends).astype(jnp.int32)
    table = jnp.transpose(expert_of.reshape(EXPERTS, TOP, TOK_DEV), (0, 2, 1))
    shuffles = jax.vmap(lambda sub_key: jax.random.permutation(sub_key, TOK_DEV))(jax.random.split(keys[4], EXPERTS)).astype(jnp.int32)
    table = jnp.take_along_axis(table, shuffles[:, :, None], axis=1)
    return table.reshape(TOKENS, TOP).astype(jnp.int32)


def shard_levels(stream_key, extent, cuts, smallest, largest):
    loudness = 1.0
    for position, shards_of in cuts:
        draws = jax.random.uniform(jax.random.fold_in(jax.random.fold_in(stream_key, 6), position), (shards_of,), jnp.float32, smallest / len(cuts), largest / len(cuts))
        loudness = loudness * jnp.repeat(jnp.exp(draws), extent[position] // shards_of).reshape((-1,) + (1,) * (len(extent) - 1 - position))
    return loudness


def centred(key, extent, spread, bound, pieces=(), kind=jnp.bfloat16):
    drawn = spread * jax.random.normal(key, extent, jnp.float32)
    if pieces:
        drawn = drawn * shard_levels(key, extent, pieces, -0.22, 0.18)
    return jnp.clip(drawn, -bound, bound).astype(kind)


def setup_inputs(seed: int = 0) -> dict:
    key_of = jax.random.split(jax.random.key(seed), 8)
    tokens_in = centred(key_of[0], (TOKENS, D), 1.0, 6.0, ((0, 32),))
    out_grad = centred(key_of[1], (TOKENS, D), 0.5, 3.0, ((0, 32),))
    expert_ids = draw_expert_ids(jax.random.fold_in(key_of[7], 71), 0)
    gate_weights = jnp.clip(jnp.exp(math.log(1.0) - 2.9957323 * jax.random.uniform(key_of[3], (TOKENS, TOP), jnp.float32) ** shard_levels(key_of[3], (TOKENS, TOP), ((0, 32),), -0.2, 0.2)), 0.05, 1.0)
    w_gate = centred(key_of[4], (EXPERTS, D, FF), D ** -0.5, 0.125, ((0, 32),))
    w_up = centred(key_of[5], (EXPERTS, D, FF), D ** -0.5, 0.125, ((0, 32),))
    w_down = centred(key_of[6], (EXPERTS, FF, D), FF ** -0.5, 0.21875, ((0, 32),))
    return {"tokens_in": tokens_in, "out_grad": out_grad, "expert_ids": expert_ids, "gate_weights": gate_weights, "w_gate": w_gate, "w_up": w_up, "w_down": w_down}


def contract_rows(first_op, second_op):
    return lax.dot_general(first_op, second_op, (((0,), (0,)), ((), ())), preferred_element_type=jnp.float32)


def contract_cols(first_op, second_op):
    return lax.dot_general(first_op, second_op, (((1,), (1,)), ((), ())), preferred_element_type=jnp.float32)


def expert_backward(inputs, grad_rows, gate_mat, up_mat, down_mat):
    gate_pre = jnp.dot(inputs, gate_mat, preferred_element_type=jnp.float32)
    up_pre = jnp.dot(inputs, up_mat, preferred_element_type=jnp.float32)
    sigma_gate = jax.nn.sigmoid(gate_pre)
    activated = gate_pre * sigma_gate
    hidden = (activated * up_pre).astype(jnp.bfloat16)
    hidden_grad = contract_cols(grad_rows, down_mat)
    down_grad = contract_rows(hidden, grad_rows).astype(jnp.bfloat16)
    gate_grad_rows = (hidden_grad * up_pre * sigma_gate * (1.0 + gate_pre * (1.0 - sigma_gate))).astype(jnp.bfloat16)
    up_grad_rows = (hidden_grad * activated).astype(jnp.bfloat16)
    input_rows = (contract_cols(gate_grad_rows, gate_mat) + contract_cols(up_grad_rows, up_mat)).astype(jnp.bfloat16)
    gate_weight_grad = contract_rows(inputs, gate_grad_rows).astype(jnp.bfloat16)
    up_weight_grad = contract_rows(inputs, up_grad_rows).astype(jnp.bfloat16)
    return gate_weight_grad, up_weight_grad, down_grad, input_rows


def reference(tokens_in, out_grad, expert_ids, gate_weights, w_gate, w_up, w_down):
    flat_ids = expert_ids.reshape(-1).astype(jnp.int32)
    sorted_rows = jnp.argsort(flat_ids, stable=True).astype(jnp.int32).reshape(EXPERTS, TOK_DEV * TOP)
    gate_flat = gate_weights.reshape(-1)

    def per_expert(summed, packed):
        pair_rows, gate_mat, up_mat, down_mat = packed
        token_rows = (pair_rows // TOP).astype(jnp.int32)
        inputs = tokens_in[token_rows]
        grad_rows = (gate_flat[pair_rows][:, None] * out_grad[token_rows].astype(jnp.float32)).astype(jnp.bfloat16)
        gate_g, up_g, down_g, input_rows = expert_backward(inputs, grad_rows, gate_mat, up_mat, down_mat)
        summed = summed.at[token_rows].add(input_rows.astype(jnp.float32))
        return summed, (gate_g, up_g, down_g)

    start_sum = jnp.zeros((TOKENS, D), jnp.float32)
    summed, grads = lax.scan(per_expert, start_sum, (sorted_rows, w_gate, w_up, w_down))
    return summed.astype(jnp.bfloat16), grads[0], grads[1], grads[2]
```

```python
import functools

import jax
import jax.numpy as jnp
from jax import lax
from jax.experimental import pallas as pl
from jax.experimental.pallas import tpu as pltpu
from jax.sharding import PartitionSpec as P

AXES = ("group", "expert")
ALIGN = 16


def contract_rows(first_op, second_op):
    return lax.dot_general(
        first_op, second_op, (((0,), (0,)), ((), ())), preferred_element_type=jnp.float32
    )


def contract_cols(first_op, second_op):
    return lax.dot_general(
        first_op, second_op, (((1,), (1,)), ((), ())), preferred_element_type=jnp.float32
    )


def expert_backward(inputs, grad_rows, gate_mat, up_mat, down_mat):
    gate_pre = jnp.dot(inputs, gate_mat, preferred_element_type=jnp.float32)
    up_pre = jnp.dot(inputs, up_mat, preferred_element_type=jnp.float32)
    sigma_gate = jax.nn.sigmoid(gate_pre)
    activated = gate_pre * sigma_gate
    hidden = (activated * up_pre).astype(jnp.bfloat16)
    hidden_grad = contract_cols(grad_rows, down_mat)
    down_grad = contract_rows(hidden, grad_rows).astype(jnp.bfloat16)
    gate_grad_rows = (
        hidden_grad * up_pre * sigma_gate * (1.0 + gate_pre * (1.0 - sigma_gate))
    ).astype(jnp.bfloat16)
    up_grad_rows = (hidden_grad * activated).astype(jnp.bfloat16)
    input_rows = (
        contract_cols(gate_grad_rows, gate_mat) + contract_cols(up_grad_rows, up_mat)
    ).astype(jnp.bfloat16)
    gate_weight_grad = contract_rows(inputs, gate_grad_rows).astype(jnp.bfloat16)
    up_weight_grad = contract_rows(inputs, up_grad_rows).astype(jnp.bfloat16)
    return (gate_weight_grad, up_weight_grad, down_grad, input_rows)


def routed(tokens_in, out_grad, expert_ids, gate_weights, w_gate, w_up, w_down):
    groups = lax.axis_size("group")
    owners = lax.axis_size("expert")
    experts = groups * owners
    token_count, top_count = expert_ids.shape
    model_width = tokens_in.shape[1]
    assigned = token_count * top_count
    capacity = 2 * assigned // experts
    flat_ids = expert_ids.reshape(assigned)
    columns = jnp.arange(experts, dtype=jnp.int32)
    counts = jnp.sum((flat_ids[:, None] == columns[None, :]).astype(jnp.int32), axis=0)
    starts = jnp.cumsum(counts) - counts
    sorted_rows = jnp.argsort(flat_ids, stable=True)
    gate_flat = gate_weights.reshape(assigned)
    sender_pos = jnp.arange(experts, dtype=jnp.int32)
    token_cols = jnp.arange(token_count, dtype=jnp.int32)
    slot_pos = jnp.arange(experts * capacity, dtype=jnp.int32)
    slot_owner = slot_pos // capacity
    slot_index = slot_pos % capacity
    filled = slot_index < counts[slot_owner]
    source = sorted_rows[jnp.minimum(starts[slot_owner] + slot_index, assigned - 1)]
    slot_token = jnp.where(filled, source // top_count, -1)
    slot_select = (slot_token[:, None] == token_cols[None, :]).astype(jnp.bfloat16)
    rows_in = jnp.dot(slot_select, tokens_in, preferred_element_type=jnp.float32).astype(
        jnp.bfloat16
    )
    picked_grad = jnp.dot(slot_select, out_grad, preferred_element_type=jnp.float32)
    rows_grad = (gate_flat[source][:, None] * picked_grad).astype(jnp.bfloat16)
    recv_in, recv_grad, recv_counts = (
        lax.all_to_all(
            rows_in.reshape(experts, capacity, model_width),
            ("group", "expert"),
            split_axis=0,
            concat_axis=0,
            tiled=True,
        ),
        lax.all_to_all(
            rows_grad.reshape(experts, capacity, model_width),
            ("group", "expert"),
            split_axis=0,
            concat_axis=0,
            tiled=True,
        ),
        lax.all_to_all(counts, ("group", "expert"), split_axis=0, concat_axis=0, tiled=True),
    )
    sender_base = sender_pos * capacity
    recv_in = recv_in.reshape(experts * capacity, model_width)
    recv_grad = recv_grad.reshape(experts * capacity, model_width)
    recv_ends = jnp.cumsum(recv_counts)
    recv_starts = recv_ends - recv_counts
    live_rows = jnp.arange(assigned, dtype=jnp.int32)
    sender = jnp.minimum(
        jnp.sum((live_rows[:, None] >= recv_ends[None, :]).astype(jnp.int32), axis=1), experts - 1
    )
    gather_rows = sender_base[sender] + live_rows - recv_starts[sender]
    inputs = recv_in[gather_rows]
    grad_rows = recv_grad[gather_rows]
    gate_weight_grad, up_weight_grad, down_grad, input_rows = expert_backward(
        inputs, grad_rows, w_gate[0], w_up[0], w_down[0]
    )
    back_slot = jnp.arange(experts * capacity, dtype=jnp.int32)
    back_off = back_slot % capacity
    back_sender = back_slot // capacity
    kept = back_off < recv_counts[back_sender]
    back_pos = jnp.minimum(recv_starts[back_sender] + back_off, assigned - 1)
    returned = jnp.where(kept[:, None], input_rows[back_pos], 0)
    arrived = lax.all_to_all(
        returned.reshape(experts, capacity, model_width),
        ("group", "expert"),
        split_axis=0,
        concat_axis=0,
        tiled=True,
    )
    arrived = arrived.reshape(experts * capacity, model_width)
    summed = contract_rows(slot_select, arrived)
    grad_in = summed.astype(jnp.bfloat16)
    return (grad_in, gate_weight_grad[None], up_weight_grad[None], down_grad[None])


def hop(value, axis, mask):
    size = lax.axis_size(axis)
    return lax.ppermute(value, axis, [(i, i ^ mask) for i in range(size)])


def after(value, *earlier):
    return lax.optimization_barrier((value, *earlier))[0]


def divisor(extent, limit):
    return next(w for w in range(limit, 0, -128) if extent % w == 0)


def slot_kernel(bounds, place, weight, *rest, sizes, first, last):
    near, far, (wg_hbm, wu_hbm, wd_hbm) = rest[:5], rest[5:10], rest[10:13]
    rest = rest[13:] if first else rest[18:]
    (x_out, g_out, h_out, gg_out, ug_out, near_sum, far_sum) = rest[:7]
    (toks, wg, wu, wd, pick, xt, gt, ht, ggt, ugt, spread, in_sem, out_sem) = rest[7:]
    model_width, hidden_width = wg.shape
    wide, slim = divisor(model_width, 512), divisor(hidden_width, 256)
    offset, count = bounds[0], bounds[1]
    tokens = near[0].shape[1]
    half = 4 * tokens
    sources = []
    for kind in range(2):
        for side, pieces in enumerate((near, far)):
            passed = pieces[3 + kind]
            parts = [p.at[kind] for p in pieces[:3]] + [passed.at[passed.shape[0] - 1]]
            for i, part in enumerate(parts):
                sources.append((part, toks.at[kind, pl.ds(side * half + i * tokens, tokens)]))
    sources += [(wd_hbm, wd), (wg_hbm, wg), (wu_hbm, wu)]
    loads = [pltpu.make_async_copy(s, d, in_sem.at[i]) for i, (s, d) in enumerate(sources)]
    for load in loads:
        load.start()

    def work(size):
        bf16, f32 = jnp.bfloat16, jnp.float32
        live = pl.ds(0, size)
        rows = lax.broadcasted_iota(jnp.int32, (size, 2 * half), 0)
        hit = place[...] == rows
        pick[live] = hit.astype(bf16)
        scale = jnp.sum(jnp.where(hit, weight[...], 0.0), axis=1, keepdims=True)

        def span(j, width):
            return pl.ds(pl.multiple_of(j * width, width), width)

        def take(source, into, factor):
            def step(j, c):
                cols = span(j, wide)
                found = jnp.dot(pick[live], toks[source, :, cols], preferred_element_type=f32)
                into[live, cols] = (found if factor is None else factor * found).astype(bf16)
                return c

            lax.fori_loop(0, model_width // wide, step, 0)

        for load in loads[:8]:
            load.wait()
        take(0, xt, None)
        for load in loads[8:16]:
            load.wait()
        take(1, gt, scale)
        for load in loads[16:]:
            load.wait()

        def forward(j, c):
            cols = span(j, slim)
            hidden_grad = contract_cols(gt[live], wd[cols, :])
            gate_pre = jnp.dot(xt[live], wg[:, cols], preferred_element_type=f32)
            up_pre = jnp.dot(xt[live], wu[:, cols], preferred_element_type=f32)
            sigma = 1.0 / (1.0 + jnp.exp(-gate_pre))
            activated = gate_pre * sigma
            ugt[live, cols] = (hidden_grad * activated).astype(bf16)
            ht[live, cols] = (activated * up_pre).astype(bf16)
            ggt[live, cols] = (
                hidden_grad * up_pre * sigma * (1.0 + gate_pre * (1.0 - sigma))
            ).astype(bf16)
            return c

        lax.fori_loop(0, hidden_width // slim, forward, 0)
        row0 = pl.multiple_of(offset, ALIGN)
        stores = [
            pltpu.make_async_copy(src.at[live], dst.at[pl.ds(row0, size)], out_sem.at[n])
            for n, (src, dst) in enumerate(
                [(xt, x_out), (gt, g_out), (ht, h_out), (ggt, gg_out), (ugt, ug_out)]
            )
        ]
        for store in stores:
            store.start()

        def back(j, c):
            cols = span(j, wide)
            found = contract_cols(ggt[live], wg[cols, :]) + contract_cols(ugt[live], wu[cols, :])
            part = contract_rows(pick[live], found.astype(bf16)).astype(bf16)
            spread[0, :, cols] = part[half:]
            spread[1, :, cols] = part[:half]
            return c

        lax.fori_loop(0, model_width // wide, back, 0)
        for n, out in enumerate((far_sum, near_sum)):
            store = pltpu.make_async_copy(spread.at[n], out, out_sem.at[5 + n])
            store.start()
            stores.append(store)
        for store in stores:
            store.wait()
        if last:
            end = pl.ds(0, last)
            stores = []
            for n, (src, dst) in enumerate(
                [(xt, x_out), (gt, g_out), (ht, h_out), (ggt, gg_out), (ugt, ug_out)]
            ):
                src[end] = jnp.zeros((last, src.shape[1]), bf16)
                into = dst.at[pl.ds(pl.multiple_of(row0 + size, ALIGN), last)]
                stores.append(pltpu.make_async_copy(src.at[end], into, out_sem.at[n]))
                stores[-1].start()
            for store in stores:
                store.wait()

    low = -1
    for size in sizes:
        pl.when((count > low) & (count <= size))(functools.partial(work, size))
        low = size


def slot_call(bounds, place, weight, near, far, weights, kept, kept_shapes, sizes, last):
    wg, wu, wd = weights
    model_width, hidden_width = wg.shape
    half = 4 * near[0].shape[1]
    bf16 = jnp.bfloat16
    anyspace = pl.BlockSpec(memory_space=pl.ANY)
    vmem = pl.BlockSpec(memory_space=pltpu.VMEM)
    smem = pl.BlockSpec(memory_space=pltpu.SMEM)
    flops = 2 * sizes[0] * model_width * (5 * hidden_width + 6 * half)
    return pl.pallas_call(
        functools.partial(slot_kernel, sizes=sizes, first=not kept, last=last),
        out_shape=[jax.ShapeDtypeStruct(shape, bf16) for shape in kept_shapes]
        + [jax.ShapeDtypeStruct((half, model_width), bf16)] * 2,
        in_specs=[smem, vmem, vmem] + [anyspace] * (13 + len(kept)),
        out_specs=[anyspace] * 7,
        input_output_aliases={16 + n: n for n in range(len(kept))},
        scratch_shapes=[
            pltpu.VMEM((2, 2 * half, model_width), bf16),
            pltpu.VMEM((model_width, hidden_width), bf16),
            pltpu.VMEM((model_width, hidden_width), bf16),
            pltpu.VMEM((hidden_width, model_width), bf16),
            pltpu.VMEM((sizes[-1], 2 * half), bf16),
            pltpu.VMEM((sizes[-1], model_width), bf16),
            pltpu.VMEM((sizes[-1], model_width), bf16),
            pltpu.VMEM((sizes[-1], hidden_width), bf16),
            pltpu.VMEM((sizes[-1], hidden_width), bf16),
            pltpu.VMEM((sizes[-1], hidden_width), bf16),
            pltpu.VMEM((2, half, model_width), bf16),
            pltpu.SemaphoreType.DMA((19,)),
            pltpu.SemaphoreType.DMA((7,)),
        ],
        compiler_params=pltpu.CompilerParams(vmem_limit_bytes=48 * 2**20),
        cost_estimate=pl.CostEstimate(
            flops=flops, bytes_accessed=24 * 2**20, transcendentals=sizes[0] * hidden_width
        ),
    )(bounds, place, weight, *near, *far, wg, wu, wd, *kept)


def flip_to_relative(value, axis, axis_name):
    me, size = lax.axis_index(axis_name), value.shape[axis]
    bit = 1
    while bit < size:
        shape = value.shape
        split = shape[:axis] + (size // (2 * bit), 2, bit) + shape[axis + 1 :]
        whole = value.reshape(split)
        value = jnp.where((me & bit) != 0, jnp.flip(whole, axis + 1), whole).reshape(shape)
        bit *= 2
    return value


def gathered(tokens_in, out_grad, expert_ids, gate_weights, w_gate, w_up, w_down):
    groups = lax.axis_size("group")
    owners = lax.axis_size("expert")
    experts = groups * owners
    token_count, top_count = expert_ids.shape
    model_width = tokens_in.shape[1]
    hidden_width = w_gate.shape[2]
    assigned = token_count * top_count
    chips = groups // 2
    half = chips * token_count
    bf16, f32 = jnp.bfloat16, jnp.float32
    weights = (w_gate[0], w_up[0], w_down[0])

    own = jnp.stack([tokens_in, out_grad])
    my_owner = lax.axis_index("expert")

    mean = assigned // owners
    sizes = (mean, mean + mean // 2, 2 * mean)
    used_rows = assigned + owners * ALIGN
    kept_rows = used_rows + 2 * mean + owners * ALIGN
    kept_shapes = [(kept_rows, w) for w in (model_width,) * 2 + (hidden_width,) * 3]
    kept = []

    slots, ups, downs = [own], [own], [own]

    def carry():
        step = len(ups)
        rising = [(i, i + 1) for i in range(step - 1, owners - 1)]
        falling = [(i + 1, i) for i in range(owners - step)]
        if step > owners - step:
            value = jnp.where(my_owner >= step - 1, ups[-1], downs[-1])
            ups.append(lax.ppermute(value, "expert", rising + falling))
            downs.append(ups[-1])
        else:
            ups.append(lax.ppermute(ups[-1], "expert", rising))
            downs.append(lax.ppermute(downs[-1], "expert", falling))

    def settle():
        slot, value = len(slots), None
        for i in range(owners):
            gap = (i ^ slot) - i
            found = downs[gap] if gap > 0 else ups[-gap]
            value = found if value is None else jnp.where(my_owner == i, found, value)
        slots.append(value)

    def routing(came):
        came = came.reshape(groups, owners, token_count)
        came = flip_to_relative(flip_to_relative(came, 0, "group"), 1, "expert")
        came = came.reshape(chips, 2, owners, token_count).transpose(2, 1, 0, 3)
        weight = came.reshape(owners, 2 * half)
        mask = weight >= 0.0
        ones = mask.astype(jnp.int32)
        place = jnp.where(mask, jnp.cumsum(ones, axis=1) - 1, -1).reshape(owners, 1, 2 * half)
        counts = jnp.sum(ones, axis=1)
        ends = jnp.cumsum((counts + ALIGN - 1) // ALIGN * ALIGN)
        bounds = jnp.stack([jnp.concatenate([jnp.zeros((1,), jnp.int32), ends[:-1]]), counts], axis=1)
        return bounds, place, weight.reshape(owners, 1, 2 * half)

    hw = model_width // 2
    lo, hi = slice(0, hw), slice(hw, model_width)

    def total(slot, chip, cols):
        near_sum, far_sum = paired[slot]
        rows = slice(chip * token_count, (chip + 1) * token_count)
        return near_sum[rows, cols].astype(f32) + far_sum[rows, cols].astype(f32)

    def exchange(starting, ending):
        for_x, for_y = [], []
        for slot in starting:
            for_x += [total(slot, 1, lo), total(slot, 3, lo)]
            for_y += [total(slot, 2, hi), total(slot, 3, hi)]
        for slot in ending:
            x1, y1 = started[slot]
            for_x.append(total(slot, 1, hi) + y1[1].astype(f32))
            for_y.append(total(slot, 2, lo) + x1[1].astype(f32))
        return (
            hop(jnp.stack(for_x).astype(bf16), "group", 2),
            hop(jnp.stack(for_y).astype(bf16), "group", 4),
        )

    columns = jnp.arange(experts, dtype=jnp.int32)
    named = expert_ids[None, :, :] == columns[:, None, None]
    sent = jnp.sum(jnp.where(named, gate_weights[None], 0.0), axis=2)
    sent = jnp.where(jnp.any(named, axis=2), sent, -1.0)
    by_x, by_y, near, far = [], [], [], []
    sums, paired, started, ended, back = {}, {}, {}, {}, {}
    route, stage = None, 0
    while len(ended) < owners:
        live = {}
        if stage < owners - 1:
            carry()
        if stage <= owners:
            new = [slots[stage]] if stage < owners else []
            to_x = new + ([by_y[-1][1:2]] if stage else [])
            to_y = new + ([by_x[-1][0:1]] if stage else [])
            live["cross"] = (
                hop(jnp.concatenate(to_x), "group", 2),
                hop(jnp.concatenate(to_y), "group", 4),
            )
        if 1 <= stage <= owners:
            live["far"] = tuple(hop(v, "group", 1) for v in near[stage - 1])
        elif stage == owners + 1:
            live["far"] = tuple(hop(v, "group", 1) for v in near[stage - 1][1:])
        if stage == 0:
            route = lax.all_to_all(sent, AXES, split_axis=0, concat_axis=0, tiled=True)
        if stage == 1:
            route = routing(route)
        if 2 <= stage < owners + 2:
            slot = stage - 2
            bounds, place, weight = route
            far.append(live.pop("far"))
            pieces = [list(v[slot]) + [v[slot + 1][-1], v[slot + 1][-2]] for v in (near, far)]
            final = owners * ALIGN if slot == owners - 1 else 0
            *kept, near_sum, far_sum = slot_call(
                bounds[slot], place[slot], weight[slot], *pieces, weights, kept, kept_shapes, sizes, final
            )
            live["sums"] = (near_sum, far_sum)
        for slot, (near_sum, far_sum) in sums.items():
            if slot not in paired:
                paired[slot] = (near_sum, hop(far_sum, "group", 1))
        if stage >= owners:
            starting = [k for k in paired if k not in started]
            ending = [k for k in started if k not in ended]
            live["back"] = exchange(starting, ending)
        arrays = (live, ups, downs, slots, near, far, sums, paired, started, ended, kept, route, by_x, by_y)
        (live, ups, downs, slots, near, far, sums, paired, started, ended, kept, route, by_x, by_y) = (
            lax.optimization_barrier(arrays)
        )
        if stage <= owners:
            by_x.append(live["cross"][0])
            by_y.append(live["cross"][1])
            near.append(((slots[stage],) if stage < owners else ()) + tuple(live["cross"]))
        if stage == owners:
            near[-1] = (by_x[-1],) + near[-1]
        if stage < owners - 1:
            settle()
        if "far" in live:
            far.append(live["far"])
        if "sums" in live:
            sums[stage - 2] = live["sums"]
        if "back" in live:
            x, y = live["back"]
            for n, slot in enumerate(starting):
                started[slot] = (x[2 * n : 2 * n + 2], y[2 * n : 2 * n + 2])
            for n, slot in enumerate(ending):
                ended[slot] = (x[2 * len(starting) + n], y[2 * len(starting) + n])
                x1, y1 = started[slot]
                left = total(slot, 0, lo) + x1[0].astype(f32) + ended[slot][1].astype(f32)
                right = total(slot, 0, hi) + y1[0].astype(f32) + ended[slot][0].astype(f32)
                mine_rows = jnp.concatenate([left, right], axis=1)
                if slot:
                    mine_rows = hop(mine_rows.astype(bf16), "expert", slot).astype(f32)
                back[slot] = mine_rows
        stage += 1
    grad_in = sum(back[slot] for slot in range(owners)).astype(bf16)

    inputs, grad_rows, hidden, gate_grad_rows, up_grad_rows = [k[:used_rows] for k in kept]
    gate_weight_grad = contract_rows(inputs, gate_grad_rows).astype(bf16)
    up_weight_grad = contract_rows(inputs, up_grad_rows).astype(bf16)
    down_grad = contract_rows(hidden, grad_rows).astype(bf16)
    return (grad_in, gate_weight_grad[None], up_weight_grad[None], down_grad[None])


def body(*args):
    groups, owners = lax.axis_size("group"), lax.axis_size("expert")
    token_count, top_count = args[2].shape
    spread = groups * owners * token_count <= 4 * token_count * top_count
    square = groups.bit_count() == 1 and len(bin(groups)) == len("0b1000")
    line = owners.bit_count() == 1
    return (gathered if spread and square and line else routed)(*args)


def solution(mesh):
    rows = P(AXES, None)
    mats = P(AXES, None, None)
    return jax.shard_map(
        body,
        mesh=mesh,
        in_specs=(rows, rows, rows, rows, mats, mats, mats),
        out_specs=(rows, mats, mats, mats),
        check_vma=False,
    )
```

```python
import functools

import jax
import jax.numpy as jnp
from jax import lax
from jax.experimental import pallas as pl
from jax.experimental.pallas import tpu as pltpu
from jax.sharding import PartitionSpec as P

AXES = ("group", "expert")
ALIGN = 16


def contract_rows(first_op, second_op):
    return lax.dot_general(
        first_op, second_op, (((0,), (0,)), ((), ())), preferred_element_type=jnp.float32
    )


def contract_cols(first_op, second_op):
    return lax.dot_general(
        first_op, second_op, (((1,), (1,)), ((), ())), preferred_element_type=jnp.float32
    )


def expert_backward(inputs, grad_rows, gate_mat, up_mat, down_mat):
    gate_pre = jnp.dot(inputs, gate_mat, preferred_element_type=jnp.float32)
    up_pre = jnp.dot(inputs, up_mat, preferred_element_type=jnp.float32)
    sigma_gate = jax.nn.sigmoid(gate_pre)
    activated = gate_pre * sigma_gate
    hidden = (activated * up_pre).astype(jnp.bfloat16)
    hidden_grad = contract_cols(grad_rows, down_mat)
    down_grad = contract_rows(hidden, grad_rows).astype(jnp.bfloat16)
    gate_grad_rows = (
        hidden_grad * up_pre * sigma_gate * (1.0 + gate_pre * (1.0 - sigma_gate))
    ).astype(jnp.bfloat16)
    up_grad_rows = (hidden_grad * activated).astype(jnp.bfloat16)
    input_rows = (
        contract_cols(gate_grad_rows, gate_mat) + contract_cols(up_grad_rows, up_mat)
    ).astype(jnp.bfloat16)
    gate_weight_grad = contract_rows(inputs, gate_grad_rows).astype(jnp.bfloat16)
    up_weight_grad = contract_rows(inputs, up_grad_rows).astype(jnp.bfloat16)
    return (gate_weight_grad, up_weight_grad, down_grad, input_rows)


def routed(tokens_in, out_grad, expert_ids, gate_weights, w_gate, w_up, w_down):
    groups = lax.axis_size("group")
    owners = lax.axis_size("expert")
    experts = groups * owners
    token_count, top_count = expert_ids.shape
    model_width = tokens_in.shape[1]
    assigned = token_count * top_count
    capacity = 2 * assigned // experts
    flat_ids = expert_ids.reshape(assigned)
    columns = jnp.arange(experts, dtype=jnp.int32)
    counts = jnp.sum((flat_ids[:, None] == columns[None, :]).astype(jnp.int32), axis=0)
    starts = jnp.cumsum(counts) - counts
    sorted_rows = jnp.argsort(flat_ids, stable=True)
    gate_flat = gate_weights.reshape(assigned)
    sender_pos = jnp.arange(experts, dtype=jnp.int32)
    token_cols = jnp.arange(token_count, dtype=jnp.int32)
    slot_pos = jnp.arange(experts * capacity, dtype=jnp.int32)
    slot_owner = slot_pos // capacity
    slot_index = slot_pos % capacity
    filled = slot_index < counts[slot_owner]
    source = sorted_rows[jnp.minimum(starts[slot_owner] + slot_index, assigned - 1)]
    slot_token = jnp.where(filled, source // top_count, -1)
    slot_select = (slot_token[:, None] == token_cols[None, :]).astype(jnp.bfloat16)
    rows_in = jnp.dot(slot_select, tokens_in, preferred_element_type=jnp.float32).astype(
        jnp.bfloat16
    )
    picked_grad = jnp.dot(slot_select, out_grad, preferred_element_type=jnp.float32)
    rows_grad = (gate_flat[source][:, None] * picked_grad).astype(jnp.bfloat16)
    recv_in, recv_grad, recv_counts = (
        lax.all_to_all(
            rows_in.reshape(experts, capacity, model_width),
            ("group", "expert"),
            split_axis=0,
            concat_axis=0,
            tiled=True,
        ),
        lax.all_to_all(
            rows_grad.reshape(experts, capacity, model_width),
            ("group", "expert"),
            split_axis=0,
            concat_axis=0,
            tiled=True,
        ),
        lax.all_to_all(counts, ("group", "expert"), split_axis=0, concat_axis=0, tiled=True),
    )
    sender_base = sender_pos * capacity
    recv_in = recv_in.reshape(experts * capacity, model_width)
    recv_grad = recv_grad.reshape(experts * capacity, model_width)
    recv_ends = jnp.cumsum(recv_counts)
    recv_starts = recv_ends - recv_counts
    live_rows = jnp.arange(assigned, dtype=jnp.int32)
    sender = jnp.minimum(
        jnp.sum((live_rows[:, None] >= recv_ends[None, :]).astype(jnp.int32), axis=1), experts - 1
    )
    gather_rows = sender_base[sender] + live_rows - recv_starts[sender]
    inputs = recv_in[gather_rows]
    grad_rows = recv_grad[gather_rows]
    gate_weight_grad, up_weight_grad, down_grad, input_rows = expert_backward(
        inputs, grad_rows, w_gate[0], w_up[0], w_down[0]
    )
    back_slot = jnp.arange(experts * capacity, dtype=jnp.int32)
    back_off = back_slot % capacity
    back_sender = back_slot // capacity
    kept = back_off < recv_counts[back_sender]
    back_pos = jnp.minimum(recv_starts[back_sender] + back_off, assigned - 1)
    returned = jnp.where(kept[:, None], input_rows[back_pos], 0)
    arrived = lax.all_to_all(
        returned.reshape(experts, capacity, model_width),
        ("group", "expert"),
        split_axis=0,
        concat_axis=0,
        tiled=True,
    )
    arrived = arrived.reshape(experts * capacity, model_width)
    summed = contract_rows(slot_select, arrived)
    grad_in = summed.astype(jnp.bfloat16)
    return (grad_in, gate_weight_grad[None], up_weight_grad[None], down_grad[None])


def hop(value, axis, mask):
    size = lax.axis_size(axis)
    return lax.ppermute(value, axis, [(i, i ^ mask) for i in range(size)])


def after(value, *earlier):
    return lax.optimization_barrier((value, *earlier))[0]


def divisor(extent, limit):
    return next(w for w in range(limit, 0, -128) if extent % w == 0)


def slot_kernel(bounds, place, weight, *rest, sizes, first, last):
    near, far, (wg_hbm, wu_hbm, wd_hbm) = rest[:5], rest[5:10], rest[10:13]
    rest = rest[13:] if first else rest[18:]
    (x_out, g_out, h_out, gg_out, ug_out, near_sum, far_sum) = rest[:7]
    (toks, wg, wu, wd, pick, xt, gt, ht, ggt, ugt, spread, in_sem, out_sem) = rest[7:]
    model_width, hidden_width = wg.shape
    wide, slim = divisor(model_width, 512), divisor(hidden_width, 256)
    offset, count = bounds[0], bounds[1]
    tokens = near[0].shape[1]
    half = 4 * tokens
    sources = []
    for kind in range(2):
        for side, pieces in enumerate((near, far)):
            passed = pieces[3 + kind]
            parts = [p.at[kind] for p in pieces[:3]] + [passed.at[passed.shape[0] - 1]]
            for i, part in enumerate(parts):
                sources.append((part, toks.at[kind, pl.ds(side * half + i * tokens, tokens)]))
    sources += [(wd_hbm, wd), (wg_hbm, wg), (wu_hbm, wu)]
    loads = [pltpu.make_async_copy(s, d, in_sem.at[i]) for i, (s, d) in enumerate(sources)]
    for load in loads:
        load.start()

    def work(size):
        bf16, f32 = jnp.bfloat16, jnp.float32
        live = pl.ds(0, size)
        rows = lax.broadcasted_iota(jnp.int32, (size, 2 * half), 0)
        hit = place[...] == rows
        pick[live] = hit.astype(bf16)
        scale = jnp.sum(jnp.where(hit, weight[...], 0.0), axis=1, keepdims=True)

        def span(j, width):
            return pl.ds(pl.multiple_of(j * width, width), width)

        def take(source, into, factor):
            def step(j, c):
                cols = span(j, wide)
                found = jnp.dot(pick[live], toks[source, :, cols], preferred_element_type=f32)
                into[live, cols] = (found if factor is None else factor * found).astype(bf16)
                return c

            lax.fori_loop(0, model_width // wide, step, 0)

        for load in loads[:8]:
            load.wait()
        take(0, xt, None)
        for load in loads[8:16]:
            load.wait()
        take(1, gt, scale)
        for load in loads[16:]:
            load.wait()

        def forward(j, c):
            cols = span(j, slim)
            hidden_grad = contract_cols(gt[live], wd[cols, :])
            gate_pre = jnp.dot(xt[live], wg[:, cols], preferred_element_type=f32)
            up_pre = jnp.dot(xt[live], wu[:, cols], preferred_element_type=f32)
            sigma = 1.0 / (1.0 + jnp.exp(-gate_pre))
            activated = gate_pre * sigma
            ugt[live, cols] = (hidden_grad * activated).astype(bf16)
            ht[live, cols] = (activated * up_pre).astype(bf16)
            ggt[live, cols] = (
                hidden_grad * up_pre * sigma * (1.0 + gate_pre * (1.0 - sigma))
            ).astype(bf16)
            return c

        lax.fori_loop(0, hidden_width // slim, forward, 0)
        row0 = pl.multiple_of(offset, ALIGN)
        stores = [
            pltpu.make_async_copy(src.at[live], dst.at[pl.ds(row0, size)], out_sem.at[n])
            for n, (src, dst) in enumerate(
                [(xt, x_out), (gt, g_out), (ht, h_out), (ggt, gg_out), (ugt, ug_out)]
            )
        ]
        for store in stores:
            store.start()

        def back(j, c):
            cols = span(j, wide)
            found = contract_cols(ggt[live], wg[cols, :]) + contract_cols(ugt[live], wu[cols, :])
            part = contract_rows(pick[live], found.astype(bf16)).astype(bf16)
            spread[0, :, cols] = part[half:]
            spread[1, :, cols] = part[:half]
            return c

        lax.fori_loop(0, model_width // wide, back, 0)
        for n, out in enumerate((far_sum, near_sum)):
            store = pltpu.make_async_copy(spread.at[n], out, out_sem.at[5 + n])
            store.start()
            stores.append(store)
        for store in stores:
            store.wait()
        if last:
            end = pl.ds(0, last)
            stores = []
            for n, (src, dst) in enumerate(
                [(xt, x_out), (gt, g_out), (ht, h_out), (ggt, gg_out), (ugt, ug_out)]
            ):
                src[end] = jnp.zeros((last, src.shape[1]), bf16)
                into = dst.at[pl.ds(pl.multiple_of(row0 + size, ALIGN), last)]
                stores.append(pltpu.make_async_copy(src.at[end], into, out_sem.at[n]))
                stores[-1].start()
            for store in stores:
                store.wait()

    low = -1
    for size in sizes:
        pl.when((count > low) & (count <= size))(functools.partial(work, size))
        low = size


def slot_call(bounds, place, weight, near, far, weights, kept, kept_shapes, sizes, last):
    wg, wu, wd = weights
    model_width, hidden_width = wg.shape
    half = 4 * near[0].shape[1]
    bf16 = jnp.bfloat16
    anyspace = pl.BlockSpec(memory_space=pl.ANY)
    vmem = pl.BlockSpec(memory_space=pltpu.VMEM)
    smem = pl.BlockSpec(memory_space=pltpu.SMEM)
    flops = 2 * sizes[0] * model_width * (5 * hidden_width + 6 * half)
    return pl.pallas_call(
        functools.partial(slot_kernel, sizes=sizes, first=not kept, last=last),
        out_shape=[jax.ShapeDtypeStruct(shape, bf16) for shape in kept_shapes]
        + [jax.ShapeDtypeStruct((half, model_width), bf16)] * 2,
        in_specs=[smem, vmem, vmem] + [anyspace] * (13 + len(kept)),
        out_specs=[anyspace] * 7,
        input_output_aliases={16 + n: n for n in range(len(kept))},
        scratch_shapes=[
            pltpu.VMEM((2, 2 * half, model_width), bf16),
            pltpu.VMEM((model_width, hidden_width), bf16),
            pltpu.VMEM((model_width, hidden_width), bf16),
            pltpu.VMEM((hidden_width, model_width), bf16),
            pltpu.VMEM((sizes[-1], 2 * half), bf16),
            pltpu.VMEM((sizes[-1], model_width), bf16),
            pltpu.VMEM((sizes[-1], model_width), bf16),
            pltpu.VMEM((sizes[-1], hidden_width), bf16),
            pltpu.VMEM((sizes[-1], hidden_width), bf16),
            pltpu.VMEM((sizes[-1], hidden_width), bf16),
            pltpu.VMEM((2, half, model_width), bf16),
            pltpu.SemaphoreType.DMA((19,)),
            pltpu.SemaphoreType.DMA((7,)),
        ],
        compiler_params=pltpu.CompilerParams(vmem_limit_bytes=48 * 2**20),
        cost_estimate=pl.CostEstimate(
            flops=flops, bytes_accessed=24 * 2**20, transcendentals=sizes[0] * hidden_width
        ),
    )(bounds, place, weight, *near, *far, wg, wu, wd, *kept)


def assemble(block, by_x, by_y):
    if not by_x:
        return block, block
    return jnp.concatenate([block, by_y[-1][1:2]]), jnp.concatenate([block, by_x[-1][0:1]])


def flip_to_relative(value, axis, axis_name):
    me, size = lax.axis_index(axis_name), value.shape[axis]
    bit = 1
    while bit < size:
        shape = value.shape
        split = shape[:axis] + (size // (2 * bit), 2, bit) + shape[axis + 1 :]
        whole = value.reshape(split)
        value = jnp.where((me & bit) != 0, jnp.flip(whole, axis + 1), whole).reshape(shape)
        bit *= 2
    return value


def gathered(tokens_in, out_grad, expert_ids, gate_weights, w_gate, w_up, w_down):
    groups = lax.axis_size("group")
    owners = lax.axis_size("expert")
    experts = groups * owners
    token_count, top_count = expert_ids.shape
    model_width = tokens_in.shape[1]
    hidden_width = w_gate.shape[2]
    assigned = token_count * top_count
    chips = groups // 2
    half = chips * token_count
    bf16, f32 = jnp.bfloat16, jnp.float32
    weights = (w_gate[0], w_up[0], w_down[0])

    own = jnp.stack([tokens_in, out_grad])
    my_owner = lax.axis_index("expert")

    mean = assigned // owners
    sizes = (mean, mean + mean // 2, 2 * mean)
    used_rows = assigned + owners * ALIGN
    kept_rows = used_rows + 2 * mean + owners * ALIGN
    kept_shapes = [(kept_rows, w) for w in (model_width,) * 2 + (hidden_width,) * 3]
    kept = []

    slots, ups, downs = [own], [own], [own]

    def carry():
        step = len(ups)
        rising = [(i, i + 1) for i in range(step - 1, owners - 1)]
        falling = [(i + 1, i) for i in range(owners - step)]
        if step > owners - step:
            value = jnp.where(my_owner >= step - 1, ups[-1], downs[-1])
            ups.append(lax.ppermute(value, "expert", rising + falling))
            downs.append(ups[-1])
        else:
            ups.append(lax.ppermute(ups[-1], "expert", rising))
            downs.append(lax.ppermute(downs[-1], "expert", falling))

    def settle():
        slot, value = len(slots), None
        for i in range(owners):
            gap = (i ^ slot) - i
            found = downs[gap] if gap > 0 else ups[-gap]
            value = found if value is None else jnp.where(my_owner == i, found, value)
        slots.append(value)

    def routing(came):
        came = came.reshape(groups, owners, token_count)
        came = flip_to_relative(flip_to_relative(came, 0, "group"), 1, "expert")
        came = came.reshape(chips, 2, owners, token_count).transpose(2, 1, 0, 3)
        weight = came.reshape(owners, 2 * half)
        mask = weight >= 0.0
        ones = mask.astype(jnp.int32)
        place = jnp.where(mask, jnp.cumsum(ones, axis=1) - 1, -1).reshape(owners, 1, 2 * half)
        counts = jnp.sum(ones, axis=1)
        ends = jnp.cumsum((counts + ALIGN - 1) // ALIGN * ALIGN)
        bounds = jnp.stack([jnp.concatenate([jnp.zeros((1,), jnp.int32), ends[:-1]]), counts], axis=1)
        return bounds, place, weight.reshape(owners, 1, 2 * half)

    hw = model_width // 2
    lo, hi = slice(0, hw), slice(hw, model_width)

    def total(slot, chip, cols):
        near_sum, far_sums = paired[slot]
        rows = slice(chip * token_count, (chip + 1) * token_count)
        whose = [c for c, count in enumerate(v.shape[0] // token_count for v in far_sums) for _ in range(count)]
        which = whose[chip]
        first = (chip - whose.index(which)) * token_count
        came = far_sums[which][first : first + token_count, cols]
        return near_sum[rows, cols].astype(f32) + came.astype(f32)

    def first_half(slot):
        for_x = jnp.concatenate([total(slot, 1, lo), total(slot, 3, lo)], axis=1)
        for_y = jnp.concatenate([total(slot, 2, hi), total(slot, 3, hi)], axis=1)
        return for_x.astype(bf16), for_y.astype(bf16)

    def second_half(slots_):
        for_x = [total(k, 1, hi) + started[k][1][:, hw:].astype(f32) for k in slots_]
        for_y = [total(k, 2, lo) + started[k][0][:, hw:].astype(f32) for k in slots_]
        return for_x, for_y

    def both(for_x, for_y):
        return hop(for_x, "group", 2), hop(for_y, "group", 4)

    columns = jnp.arange(experts, dtype=jnp.int32)
    named = expert_ids[None, :, :] == columns[:, None, None]
    sent = jnp.sum(jnp.where(named, gate_weights[None], 0.0), axis=2)
    sent = jnp.where(jnp.any(named, axis=2), sent, -1.0)
    by_x, by_y, near, far = [], [], [], []
    paired, started, back = {}, {}, {}
    early, late = list(range(owners - 2)), owners - 2
    route, grads = None, []
    for stage in range(owners + 3):
        new = {}
        if stage < owners:
            new["cross"] = both(*assemble(slots[stage], by_x, by_y))
        elif stage == owners:
            starts = [first_half(k) for k in early] + [(by_y[-1][1], by_x[-1][0])]
            new["cross"] = both(*[jnp.stack(v) for v in zip(*starts)])
        if stage < owners - 1:
            carry()
            settle()
        if stage > owners:
            slot = stage - 3
            if stage == owners + 2:
                near_sum, (far_own, far_rest) = paired[slot]
                paired[slot] = (near_sum, (far_own, hop(far_rest, "group", 1)))
            for_x = [total(slot, 1, lo), total(slot, 1, hi)]
            for_y = [total(slot, 2, lo), total(slot, 2, hi)]
            if slot == late:
                rest_x, rest_y = second_half(early)
                for_x, for_y = for_x + rest_x, for_y + rest_y
            sends = (jnp.stack(for_x).astype(bf16), jnp.stack(for_y).astype(bf16))
            sends += (total(slot, 3, slice(None)).astype(bf16),)
            new["straight"] = both(*sends[:2])
            new["corner"] = hop(sends[2], "group", 6)
            if stage == owners + 2:
                far_own = hop(after(far_own, *sends), "group", 1)
                paired[slot] = (near_sum, (far_own, paired[slot][1][1]))
                going, rows = after(({k: back[k] for k in back if k}, kept), far_own)
                new["home"] = {k: hop(going[k].astype(bf16), "expert", k) for k in going}
                rows = [k[:used_rows] for k in rows]
                grads = [contract_rows(rows[0], rows[n]).astype(bf16) for n in (3, 4)]
        if 1 <= stage <= owners:
            mine = near[stage - 1]
            if stage == 1:
                mine = after(mine, ups[-1], downs[-1])
            new["far"] = tuple(hop(v, "group", 1) for v in mine)
        elif stage == owners + 1:
            new["far"] = tuple(hop(v, "group", 1) for v in after(near[stage - 1], *sends))
        if stage == 0:
            route = lax.all_to_all(sent, AXES, split_axis=0, concat_axis=0, tiled=True)
        if stage == 1:
            route = routing(after(route, ups[-1], downs[-1]))
        if 2 <= stage < owners + 2:
            slot = stage - 2
            bounds, place, weight = route
            far.append(new.pop("far"))
            pieces = [list(v[slot]) + [v[slot + 1][-1], v[slot + 1][-2]] for v in (near, far)]
            final = owners * ALIGN if slot == owners - 1 else 0
            *kept, near_sum, far_sum = slot_call(
                bounds[slot], place[slot], weight[slot], *pieces, weights, kept, kept_shapes, sizes, final
            )
            cut = far_sum.shape[0] // 2 if slot < owners - 1 else token_count
            far_sums = (far_sum[:cut], far_sum[cut:])
            if slot < owners - 1:
                far_sums = tuple(hop(v, "group", 1) for v in far_sums)
            new["paired"] = (near_sum, far_sums)
        arrays = (new, ups, downs, slots, near, far, paired, started, back, kept, route, grads, by_x, by_y)
        new, ups, downs, slots, near, far, paired, started, back, kept, route, grads, by_x, by_y = (
            lax.optimization_barrier(arrays)
        )
        if "cross" in new:
            x, y = new["cross"]
            if stage < owners:
                by_x.append(x)
                by_y.append(y)
                near.append((slots[stage], x, y))
            else:
                near.append((x[-1:], y[-1:]))
                started = {k: (x[k], y[k]) for k in early}
        if "far" in new:
            far.append(new["far"])
        if "paired" in new:
            paired[stage - 2] = new["paired"]
        if "straight" in new:
            slot = stage - 3
            x, y = [v.astype(f32) for v in new["straight"]]
            back[slot] = total(slot, 0, slice(None)) + new["corner"].astype(f32)
            back[slot] += jnp.concatenate([x[0] + y[0], x[1] + y[1]], axis=1)
            if slot == late:
                for k in early:
                    left = total(k, 0, lo) + started[k][0][:, :hw].astype(f32) + y[2 + k]
                    right = total(k, 0, hi) + started[k][1][:, :hw].astype(f32) + x[2 + k]
                    back[k] = jnp.concatenate([left, right], axis=1)
        if "home" in new:
            back.update(new["home"])
    last = owners - 1
    back[last] = hop(back[last].astype(bf16), "expert", last)
    grad_in = sum(back[slot].astype(f32) for slot in range(owners)).astype(bf16)

    hidden, grad_rows = kept[2][:used_rows], kept[1][:used_rows]
    gate_weight_grad, up_weight_grad = grads
    down_grad = contract_rows(hidden, grad_rows).astype(bf16)
    return (grad_in, gate_weight_grad[None], up_weight_grad[None], down_grad[None])


def body(*args):
    groups, owners = lax.axis_size("group"), lax.axis_size("expert")
    token_count, top_count = args[2].shape
    spread = groups * owners * token_count <= 4 * token_count * top_count
    square = groups.bit_count() == 1 and len(bin(groups)) == len("0b1000")
    line = owners > 2 and owners.bit_count() == 1
    return (gathered if spread and square and line else routed)(*args)


def solution(mesh):
    rows = P(AXES, None)
    mats = P(AXES, None, None)
    return jax.shard_map(
        body,
        mesh=mesh,
        in_specs=(rows, rows, rows, rows, mats, mats, mats),
        out_specs=(rows, mats, mats, mats),
        check_vma=False,
    )
```

```python
import functools

import jax
import jax.numpy as jnp
from jax import lax
from jax.experimental import pallas as pl
from jax.experimental.pallas import tpu as pltpu
from jax.sharding import PartitionSpec as P

AXES = ("group", "expert")
ALIGN = 16


def contract_rows(first_op, second_op):
    return lax.dot_general(
        first_op, second_op, (((0,), (0,)), ((), ())), preferred_element_type=jnp.float32
    )


def contract_cols(first_op, second_op):
    return lax.dot_general(
        first_op, second_op, (((1,), (1,)), ((), ())), preferred_element_type=jnp.float32
    )


def expert_backward(inputs, grad_rows, gate_mat, up_mat, down_mat):
    gate_pre = jnp.dot(inputs, gate_mat, preferred_element_type=jnp.float32)
    up_pre = jnp.dot(inputs, up_mat, preferred_element_type=jnp.float32)
    sigma_gate = jax.nn.sigmoid(gate_pre)
    activated = gate_pre * sigma_gate
    hidden = (activated * up_pre).astype(jnp.bfloat16)
    hidden_grad = contract_cols(grad_rows, down_mat)
    down_grad = contract_rows(hidden, grad_rows).astype(jnp.bfloat16)
    gate_grad_rows = (
        hidden_grad * up_pre * sigma_gate * (1.0 + gate_pre * (1.0 - sigma_gate))
    ).astype(jnp.bfloat16)
    up_grad_rows = (hidden_grad * activated).astype(jnp.bfloat16)
    input_rows = (
        contract_cols(gate_grad_rows, gate_mat) + contract_cols(up_grad_rows, up_mat)
    ).astype(jnp.bfloat16)
    gate_weight_grad = contract_rows(inputs, gate_grad_rows).astype(jnp.bfloat16)
    up_weight_grad = contract_rows(inputs, up_grad_rows).astype(jnp.bfloat16)
    return (gate_weight_grad, up_weight_grad, down_grad, input_rows)


def routed(tokens_in, out_grad, expert_ids, gate_weights, w_gate, w_up, w_down):
    groups = lax.axis_size("group")
    owners = lax.axis_size("expert")
    experts = groups * owners
    token_count, top_count = expert_ids.shape
    model_width = tokens_in.shape[1]
    assigned = token_count * top_count
    capacity = 2 * assigned // experts
    flat_ids = expert_ids.reshape(assigned)
    columns = jnp.arange(experts, dtype=jnp.int32)
    counts = jnp.sum((flat_ids[:, None] == columns[None, :]).astype(jnp.int32), axis=0)
    starts = jnp.cumsum(counts) - counts
    sorted_rows = jnp.argsort(flat_ids, stable=True)
    gate_flat = gate_weights.reshape(assigned)
    sender_pos = jnp.arange(experts, dtype=jnp.int32)
    token_cols = jnp.arange(token_count, dtype=jnp.int32)
    slot_pos = jnp.arange(experts * capacity, dtype=jnp.int32)
    slot_owner = slot_pos // capacity
    slot_index = slot_pos % capacity
    filled = slot_index < counts[slot_owner]
    source = sorted_rows[jnp.minimum(starts[slot_owner] + slot_index, assigned - 1)]
    slot_token = jnp.where(filled, source // top_count, -1)
    slot_select = (slot_token[:, None] == token_cols[None, :]).astype(jnp.bfloat16)
    rows_in = jnp.dot(slot_select, tokens_in, preferred_element_type=jnp.float32).astype(
        jnp.bfloat16
    )
    picked_grad = jnp.dot(slot_select, out_grad, preferred_element_type=jnp.float32)
    rows_grad = (gate_flat[source][:, None] * picked_grad).astype(jnp.bfloat16)
    recv_in, recv_grad, recv_counts = (
        lax.all_to_all(
            rows_in.reshape(experts, capacity, model_width),
            ("group", "expert"),
            split_axis=0,
            concat_axis=0,
            tiled=True,
        ),
        lax.all_to_all(
            rows_grad.reshape(experts, capacity, model_width),
            ("group", "expert"),
            split_axis=0,
            concat_axis=0,
            tiled=True,
        ),
        lax.all_to_all(counts, ("group", "expert"), split_axis=0, concat_axis=0, tiled=True),
    )
    sender_base = sender_pos * capacity
    recv_in = recv_in.reshape(experts * capacity, model_width)
    recv_grad = recv_grad.reshape(experts * capacity, model_width)
    recv_ends = jnp.cumsum(recv_counts)
    recv_starts = recv_ends - recv_counts
    live_rows = jnp.arange(assigned, dtype=jnp.int32)
    sender = jnp.minimum(
        jnp.sum((live_rows[:, None] >= recv_ends[None, :]).astype(jnp.int32), axis=1), experts - 1
    )
    gather_rows = sender_base[sender] + live_rows - recv_starts[sender]
    inputs = recv_in[gather_rows]
    grad_rows = recv_grad[gather_rows]
    gate_weight_grad, up_weight_grad, down_grad, input_rows = expert_backward(
        inputs, grad_rows, w_gate[0], w_up[0], w_down[0]
    )
    back_slot = jnp.arange(experts * capacity, dtype=jnp.int32)
    back_off = back_slot % capacity
    back_sender = back_slot // capacity
    kept = back_off < recv_counts[back_sender]
    back_pos = jnp.minimum(recv_starts[back_sender] + back_off, assigned - 1)
    returned = jnp.where(kept[:, None], input_rows[back_pos], 0)
    arrived = lax.all_to_all(
        returned.reshape(experts, capacity, model_width),
        ("group", "expert"),
        split_axis=0,
        concat_axis=0,
        tiled=True,
    )
    arrived = arrived.reshape(experts * capacity, model_width)
    summed = contract_rows(slot_select, arrived)
    grad_in = summed.astype(jnp.bfloat16)
    return (grad_in, gate_weight_grad[None], up_weight_grad[None], down_grad[None])


def hop(value, axis, mask):
    size = lax.axis_size(axis)
    return lax.ppermute(value, axis, [(i, i ^ mask) for i in range(size)])


def after(value, *earlier):
    return lax.optimization_barrier((value, *earlier))[0]


def divisor(extent, limit):
    return next(w for w in range(limit, 0, -128) if extent % w == 0)


def slot_kernel(bounds, place, weight, *rest, sizes, first, last):
    near, far, (wg_hbm, wu_hbm, wd_hbm) = rest[:5], rest[5:10], rest[10:13]
    rest = rest[13:] if first else rest[18:]
    (x_out, g_out, h_out, gg_out, ug_out, near_sum, far_sum) = rest[:7]
    (toks, wg, wu, wd, pick, xt, gt, ht, ggt, ugt, spread, in_sem, out_sem) = rest[7:]
    model_width, hidden_width = wg.shape
    wide, slim = divisor(model_width, 512), divisor(hidden_width, 256)
    offset, count = bounds[0], bounds[1]
    tokens = near[0].shape[1]
    half = 4 * tokens
    sources = []
    for kind in range(2):
        for side, pieces in enumerate((near, far)):
            passed = pieces[3 + kind]
            parts = [p.at[kind] for p in pieces[:3]] + [passed.at[passed.shape[0] - 1]]
            for i, part in enumerate(parts):
                sources.append((part, toks.at[kind, pl.ds(side * half + i * tokens, tokens)]))
    sources += [(wd_hbm, wd), (wg_hbm, wg), (wu_hbm, wu)]
    loads = [pltpu.make_async_copy(s, d, in_sem.at[i]) for i, (s, d) in enumerate(sources)]
    for load in loads:
        load.start()

    def work(size):
        bf16, f32 = jnp.bfloat16, jnp.float32
        live = pl.ds(0, size)
        rows = lax.broadcasted_iota(jnp.int32, (size, 2 * half), 0)
        hit = place[...] == rows
        pick[live] = hit.astype(bf16)
        scale = jnp.sum(jnp.where(hit, weight[...], 0.0), axis=1, keepdims=True)

        def span(j, width):
            return pl.ds(pl.multiple_of(j * width, width), width)

        def take(source, into, factor):
            def step(j, c):
                cols = span(j, wide)
                found = jnp.dot(pick[live], toks[source, :, cols], preferred_element_type=f32)
                into[live, cols] = (found if factor is None else factor * found).astype(bf16)
                return c

            lax.fori_loop(0, model_width // wide, step, 0)

        for load in loads[:8]:
            load.wait()
        take(0, xt, None)
        for load in loads[8:16]:
            load.wait()
        take(1, gt, scale)
        for load in loads[16:]:
            load.wait()

        def forward(j, c):
            cols = span(j, slim)
            hidden_grad = contract_cols(gt[live], wd[cols, :])
            gate_pre = jnp.dot(xt[live], wg[:, cols], preferred_element_type=f32)
            up_pre = jnp.dot(xt[live], wu[:, cols], preferred_element_type=f32)
            sigma = 1.0 / (1.0 + jnp.exp(-gate_pre))
            activated = gate_pre * sigma
            ugt[live, cols] = (hidden_grad * activated).astype(bf16)
            ht[live, cols] = (activated * up_pre).astype(bf16)
            ggt[live, cols] = (
                hidden_grad * up_pre * sigma * (1.0 + gate_pre * (1.0 - sigma))
            ).astype(bf16)
            return c

        lax.fori_loop(0, hidden_width // slim, forward, 0)
        row0 = pl.multiple_of(offset, ALIGN)
        stores = [
            pltpu.make_async_copy(src.at[live], dst.at[pl.ds(row0, size)], out_sem.at[n])
            for n, (src, dst) in enumerate(
                [(xt, x_out), (gt, g_out), (ht, h_out), (ggt, gg_out), (ugt, ug_out)]
            )
        ]
        for store in stores:
            store.start()

        def back(j, c):
            cols = span(j, wide)
            found = contract_cols(ggt[live], wg[cols, :]) + contract_cols(ugt[live], wu[cols, :])
            part = contract_rows(pick[live], found.astype(bf16)).astype(bf16)
            spread[0, :, cols] = part[half:]
            spread[1, :, cols] = part[:half]
            return c

        lax.fori_loop(0, model_width // wide, back, 0)
        for n, out in enumerate((far_sum, near_sum)):
            store = pltpu.make_async_copy(spread.at[n], out, out_sem.at[5 + n])
            store.start()
            stores.append(store)
        for store in stores:
            store.wait()
        if last:
            end = pl.ds(0, last)
            stores = []
            for n, (src, dst) in enumerate(
                [(xt, x_out), (gt, g_out), (ht, h_out), (ggt, gg_out), (ugt, ug_out)]
            ):
                src[end] = jnp.zeros((last, src.shape[1]), bf16)
                into = dst.at[pl.ds(pl.multiple_of(row0 + size, ALIGN), last)]
                stores.append(pltpu.make_async_copy(src.at[end], into, out_sem.at[n]))
                stores[-1].start()
            for store in stores:
                store.wait()

    low = -1
    for size in sizes:
        pl.when((count > low) & (count <= size))(functools.partial(work, size))
        low = size


def slot_call(bounds, place, weight, near, far, weights, kept, kept_shapes, sizes, last):
    wg, wu, wd = weights
    model_width, hidden_width = wg.shape
    half = 4 * near[0].shape[1]
    bf16 = jnp.bfloat16
    anyspace = pl.BlockSpec(memory_space=pl.ANY)
    vmem = pl.BlockSpec(memory_space=pltpu.VMEM)
    smem = pl.BlockSpec(memory_space=pltpu.SMEM)
    flops = 2 * sizes[0] * model_width * (5 * hidden_width + 6 * half)
    return pl.pallas_call(
        functools.partial(slot_kernel, sizes=sizes, first=not kept, last=last),
        out_shape=[jax.ShapeDtypeStruct(shape, bf16) for shape in kept_shapes]
        + [jax.ShapeDtypeStruct((half, model_width), bf16)] * 2,
        in_specs=[smem, vmem, vmem] + [anyspace] * (13 + len(kept)),
        out_specs=[anyspace] * 7,
        input_output_aliases={16 + n: n for n in range(len(kept))},
        scratch_shapes=[
            pltpu.VMEM((2, 2 * half, model_width), bf16),
            pltpu.VMEM((model_width, hidden_width), bf16),
            pltpu.VMEM((model_width, hidden_width), bf16),
            pltpu.VMEM((hidden_width, model_width), bf16),
            pltpu.VMEM((sizes[-1], 2 * half), bf16),
            pltpu.VMEM((sizes[-1], model_width), bf16),
            pltpu.VMEM((sizes[-1], model_width), bf16),
            pltpu.VMEM((sizes[-1], hidden_width), bf16),
            pltpu.VMEM((sizes[-1], hidden_width), bf16),
            pltpu.VMEM((sizes[-1], hidden_width), bf16),
            pltpu.VMEM((2, half, model_width), bf16),
            pltpu.SemaphoreType.DMA((19,)),
            pltpu.SemaphoreType.DMA((7,)),
        ],
        compiler_params=pltpu.CompilerParams(vmem_limit_bytes=48 * 2**20),
        cost_estimate=pl.CostEstimate(
            flops=flops, bytes_accessed=24 * 2**20, transcendentals=sizes[0] * hidden_width
        ),
    )(bounds, place, weight, *near, *far, wg, wu, wd, *kept)


def assemble(block, by_x, by_y):
    if not by_x:
        return block, block
    return jnp.concatenate([block, by_y[-1][1:2]]), jnp.concatenate([block, by_x[-1][0:1]])


def flip_to_relative(value, axis, axis_name):
    me, size = lax.axis_index(axis_name), value.shape[axis]
    bit = 1
    while bit < size:
        shape = value.shape
        split = shape[:axis] + (size // (2 * bit), 2, bit) + shape[axis + 1 :]
        whole = value.reshape(split)
        value = jnp.where((me & bit) != 0, jnp.flip(whole, axis + 1), whole).reshape(shape)
        bit *= 2
    return value


def gathered(tokens_in, out_grad, expert_ids, gate_weights, w_gate, w_up, w_down):
    groups = lax.axis_size("group")
    owners = lax.axis_size("expert")
    experts = groups * owners
    token_count, top_count = expert_ids.shape
    model_width = tokens_in.shape[1]
    hidden_width = w_gate.shape[2]
    assigned = token_count * top_count
    chips = groups // 2
    half = chips * token_count
    bf16, f32 = jnp.bfloat16, jnp.float32
    weights = (w_gate[0], w_up[0], w_down[0])

    own = jnp.stack([tokens_in, out_grad])
    my_owner = lax.axis_index("expert")

    mean = assigned // owners
    sizes = (mean, mean + mean // 2, 2 * mean)
    used_rows = assigned + owners * ALIGN
    kept_rows = used_rows + 2 * mean + owners * ALIGN
    kept_shapes = [(kept_rows, w) for w in (model_width,) * 2 + (hidden_width,) * 3]
    kept = []

    slots, ups, downs = [own], [own], [own]

    def carry():
        step = len(ups)
        rising = [(i, i + 1) for i in range(step - 1, owners - 1)]
        falling = [(i + 1, i) for i in range(owners - step)]
        if step > owners - step:
            value = jnp.where(my_owner >= step - 1, ups[-1], downs[-1])
            ups.append(lax.ppermute(value, "expert", rising + falling))
            downs.append(ups[-1])
        else:
            ups.append(lax.ppermute(ups[-1], "expert", rising))
            downs.append(lax.ppermute(downs[-1], "expert", falling))

    def settle():
        slot, value = len(slots), None
        for i in range(owners):
            gap = (i ^ slot) - i
            found = downs[gap] if gap > 0 else ups[-gap]
            value = found if value is None else jnp.where(my_owner == i, found, value)
        slots.append(value)

    def routing(came):
        came = came.reshape(groups, owners, token_count)
        came = flip_to_relative(flip_to_relative(came, 0, "group"), 1, "expert")
        came = came.reshape(chips, 2, owners, token_count).transpose(2, 1, 0, 3)
        weight = came.reshape(owners, 2 * half)
        mask = weight >= 0.0
        ones = mask.astype(jnp.int32)
        place = jnp.where(mask, jnp.cumsum(ones, axis=1) - 1, -1).reshape(owners, 1, 2 * half)
        counts = jnp.sum(ones, axis=1)
        ends = jnp.cumsum((counts + ALIGN - 1) // ALIGN * ALIGN)
        bounds = jnp.stack([jnp.concatenate([jnp.zeros((1,), jnp.int32), ends[:-1]]), counts], axis=1)
        return bounds, place, weight.reshape(owners, 1, 2 * half)

    hw = model_width // 2
    lo, hi = slice(0, hw), slice(hw, model_width)

    def total(slot, chip, cols):
        near_sum, far_sums = paired[slot]
        rows = slice(chip * token_count, (chip + 1) * token_count)
        whose = [c for c, count in enumerate(v.shape[0] // token_count for v in far_sums) for _ in range(count)]
        which = whose[chip]
        first = (chip - whose.index(which)) * token_count
        came = far_sums[which][first : first + token_count, cols]
        return near_sum[rows, cols].astype(f32) + came.astype(f32)

    def first_half(slot):
        for_x = jnp.concatenate([total(slot, 1, lo), total(slot, 3, lo)], axis=1)
        for_y = jnp.concatenate([total(slot, 2, hi), total(slot, 3, hi)], axis=1)
        return for_x.astype(bf16), for_y.astype(bf16)

    def second_half(slots_):
        for_x = [total(k, 1, hi) + started[1][k, :, hw:].astype(f32) for k in slots_]
        for_y = [total(k, 2, lo) + started[0][k, :, hw:].astype(f32) for k in slots_]
        return tuple(
            jnp.stack([jnp.concatenate(v[n : n + 2], axis=1) for n in range(0, len(v), 2)]).astype(bf16)
            for v in (for_x, for_y)
        )

    def both(for_x, for_y):
        return hop(for_x, "group", 2), hop(for_y, "group", 4)

    columns = jnp.arange(experts, dtype=jnp.int32)
    named = expert_ids[None, :, :] == columns[:, None, None]
    sent = jnp.sum(jnp.where(named, gate_weights[None], 0.0), axis=2)
    sent = jnp.where(jnp.any(named, axis=2), sent, -1.0)
    by_x, by_y, near, far = [], [], [], []
    paired, started, back = {}, (), {}
    early, late = list(range(owners - 2)), owners - 2
    route, grads = None, []
    for stage in range(owners + 3):
        new = {}
        if stage < owners:
            pair = assemble(slots[stage], by_x, by_y)
            new["cross"] = both(*pair)
            if 0 < stage < owners - 1:
                ups[-1], downs[-1] = after((ups[-1], downs[-1]), *pair)
        elif stage == owners:
            starts = [first_half(k) for k in early] + [(by_y[-1][1], by_x[-1][0])]
            new["cross"] = both(*[jnp.stack(v) for v in zip(*starts)])
        if stage < owners - 1:
            carry()
            settle()
        if stage > owners:
            slot = stage - 3
            if stage == owners + 2:
                near_sum, (far_own, far_rest) = paired[slot]
                paired[slot] = (near_sum, (far_own, hop(far_rest, "group", 1)))
            sends = tuple(total(slot, chip, slice(None)).astype(bf16)[None] for chip in (1, 2))
            if slot == late:
                sends = tuple(jnp.concatenate(v) for v in zip(sends, second_half(early)))
            sends += (total(slot, 3, slice(None)).astype(bf16),)
            new["straight"] = both(*sends[:2])
            new["corner"] = hop(sends[2], "group", 6)
            if stage == owners + 2:
                far_own = hop(after(far_own, *sends), "group", 1)
                paired[slot] = (near_sum, (far_own, paired[slot][1][1]))
                going, rows = after(({k: back[k] for k in back if k}, kept), far_own)
                new["home"] = {k: hop(going[k].astype(bf16), "expert", k) for k in going}
                rows = [k[:used_rows] for k in rows]
                grads = [contract_rows(rows[0], rows[n]).astype(bf16) for n in (3, 4)]
        if 1 <= stage <= owners:
            mine = near[stage - 1]
            if stage == 1:
                mine = after(mine, ups[-1], downs[-1])
            new["far"] = tuple(hop(v, "group", 1) for v in mine)
        elif stage == owners + 1:
            near[owners] = tuple(v[-1:] for v in after(near[owners], *sends))
            new["far"] = tuple(hop(v, "group", 1) for v in near[owners])
        if stage == 0:
            route = lax.all_to_all(sent, AXES, split_axis=0, concat_axis=0, tiled=True)
        if stage == 1:
            route = routing(after(route, ups[-1], downs[-1]))
        if 2 <= stage < owners + 2:
            slot = stage - 2
            bounds, place, weight = route
            far.append(new.pop("far"))
            pieces = [list(v[slot]) + [v[slot + 1][-1], v[slot + 1][-2]] for v in (near, far)]
            final = owners * ALIGN if slot == owners - 1 else 0
            *kept, near_sum, far_sum = slot_call(
                bounds[slot], place[slot], weight[slot], *pieces, weights, kept, kept_shapes, sizes, final
            )
            cut = far_sum.shape[0] // 2 if slot < owners - 1 else token_count
            far_sums = (far_sum[:cut], far_sum[cut:])
            if slot < owners - 1:
                far_sums = tuple(hop(v, "group", 1) for v in far_sums)
            new["paired"] = (near_sum, far_sums)
        arrays = (new, ups, downs, slots, near, far, paired, started, back, kept, route, grads, by_x, by_y)
        new, ups, downs, slots, near, far, paired, started, back, kept, route, grads, by_x, by_y = (
            lax.optimization_barrier(arrays)
        )
        if "cross" in new:
            x, y = new["cross"]
            if stage < owners:
                by_x.append(x)
                by_y.append(y)
                near.append((slots[stage], x, y))
            else:
                near.append((x, y))
                started = (x, y)
        if "far" in new:
            far.append(new["far"])
        if "paired" in new:
            paired[stage - 2] = new["paired"]
        if "straight" in new:
            slot = stage - 3
            x, y = [v.astype(f32) for v in new["straight"]]
            back[slot] = total(slot, 0, slice(None)) + new["corner"].astype(f32)
            back[slot] += x[0] + y[0]
            if slot == late:
                for k in early:
                    half = slice(k % 2 * hw, (k % 2 + 1) * hw)
                    left = total(k, 0, lo) + started[0][k, :, :hw].astype(f32) + y[1 + k // 2][:, half]
                    right = total(k, 0, hi) + started[1][k, :, :hw].astype(f32) + x[1 + k // 2][:, half]
                    back[k] = jnp.concatenate([left, right], axis=1)
        if "home" in new:
            back.update(new["home"])
    last = owners - 1
    back[last] = hop(back[last].astype(bf16), "expert", last)
    grad_in = sum(back[slot].astype(f32) for slot in range(owners)).astype(bf16)

    hidden, grad_rows = kept[2][:used_rows], kept[1][:used_rows]
    gate_weight_grad, up_weight_grad = grads
    down_grad = contract_rows(hidden, grad_rows).astype(bf16)
    return (grad_in, gate_weight_grad[None], up_weight_grad[None], down_grad[None])


def body(*args):
    groups, owners = lax.axis_size("group"), lax.axis_size("expert")
    token_count, top_count = args[2].shape
    spread = groups * owners * token_count <= 4 * token_count * top_count
    square = groups.bit_count() == 1 and len(bin(groups)) == len("0b1000")
    line = owners > 2 and owners.bit_count() == 1
    return (gathered if spread and square and line else routed)(*args)


def solution(mesh):
    rows = P(AXES, None)
    mats = P(AXES, None, None)
    return jax.shard_map(
        body,
        mesh=mesh,
        in_specs=(rows, rows, rows, rows, mats, mats, mats),
        out_specs=(rows, mats, mats, mats),
        check_vma=False,
    )
```

```python
import functools

import jax
import jax.numpy as jnp
from jax import lax
from jax.experimental import pallas as pl
from jax.experimental.pallas import tpu as pltpu
from jax.sharding import PartitionSpec as P

AXES = ("group", "expert")
ALIGN = 16


def contract_rows(first_op, second_op):
    return lax.dot_general(
        first_op, second_op, (((0,), (0,)), ((), ())), preferred_element_type=jnp.float32
    )


def contract_cols(first_op, second_op):
    return lax.dot_general(
        first_op, second_op, (((1,), (1,)), ((), ())), preferred_element_type=jnp.float32
    )


def expert_backward(inputs, grad_rows, gate_mat, up_mat, down_mat):
    gate_pre = jnp.dot(inputs, gate_mat, preferred_element_type=jnp.float32)
    up_pre = jnp.dot(inputs, up_mat, preferred_element_type=jnp.float32)
    sigma_gate = jax.nn.sigmoid(gate_pre)
    activated = gate_pre * sigma_gate
    hidden = (activated * up_pre).astype(jnp.bfloat16)
    hidden_grad = contract_cols(grad_rows, down_mat)
    down_grad = contract_rows(hidden, grad_rows).astype(jnp.bfloat16)
    gate_grad_rows = (
        hidden_grad * up_pre * sigma_gate * (1.0 + gate_pre * (1.0 - sigma_gate))
    ).astype(jnp.bfloat16)
    up_grad_rows = (hidden_grad * activated).astype(jnp.bfloat16)
    input_rows = (
        contract_cols(gate_grad_rows, gate_mat) + contract_cols(up_grad_rows, up_mat)
    ).astype(jnp.bfloat16)
    gate_weight_grad = contract_rows(inputs, gate_grad_rows).astype(jnp.bfloat16)
    up_weight_grad = contract_rows(inputs, up_grad_rows).astype(jnp.bfloat16)
    return (gate_weight_grad, up_weight_grad, down_grad, input_rows)


def routed(tokens_in, out_grad, expert_ids, gate_weights, w_gate, w_up, w_down):
    groups = lax.axis_size("group")
    owners = lax.axis_size("expert")
    experts = groups * owners
    token_count, top_count = expert_ids.shape
    model_width = tokens_in.shape[1]
    assigned = token_count * top_count
    capacity = 2 * assigned // experts
    flat_ids = expert_ids.reshape(assigned)
    columns = jnp.arange(experts, dtype=jnp.int32)
    counts = jnp.sum((flat_ids[:, None] == columns[None, :]).astype(jnp.int32), axis=0)
    starts = jnp.cumsum(counts) - counts
    sorted_rows = jnp.argsort(flat_ids, stable=True)
    gate_flat = gate_weights.reshape(assigned)
    sender_pos = jnp.arange(experts, dtype=jnp.int32)
    token_cols = jnp.arange(token_count, dtype=jnp.int32)
    slot_pos = jnp.arange(experts * capacity, dtype=jnp.int32)
    slot_owner = slot_pos // capacity
    slot_index = slot_pos % capacity
    filled = slot_index < counts[slot_owner]
    source = sorted_rows[jnp.minimum(starts[slot_owner] + slot_index, assigned - 1)]
    slot_token = jnp.where(filled, source // top_count, -1)
    slot_select = (slot_token[:, None] == token_cols[None, :]).astype(jnp.bfloat16)
    rows_in = jnp.dot(slot_select, tokens_in, preferred_element_type=jnp.float32).astype(
        jnp.bfloat16
    )
    picked_grad = jnp.dot(slot_select, out_grad, preferred_element_type=jnp.float32)
    rows_grad = (gate_flat[source][:, None] * picked_grad).astype(jnp.bfloat16)
    recv_in, recv_grad, recv_counts = (
        lax.all_to_all(
            rows_in.reshape(experts, capacity, model_width),
            ("group", "expert"),
            split_axis=0,
            concat_axis=0,
            tiled=True,
        ),
        lax.all_to_all(
            rows_grad.reshape(experts, capacity, model_width),
            ("group", "expert"),
            split_axis=0,
            concat_axis=0,
            tiled=True,
        ),
        lax.all_to_all(counts, ("group", "expert"), split_axis=0, concat_axis=0, tiled=True),
    )
    sender_base = sender_pos * capacity
    recv_in = recv_in.reshape(experts * capacity, model_width)
    recv_grad = recv_grad.reshape(experts * capacity, model_width)
    recv_ends = jnp.cumsum(recv_counts)
    recv_starts = recv_ends - recv_counts
    live_rows = jnp.arange(assigned, dtype=jnp.int32)
    sender = jnp.minimum(
        jnp.sum((live_rows[:, None] >= recv_ends[None, :]).astype(jnp.int32), axis=1), experts - 1
    )
    gather_rows = sender_base[sender] + live_rows - recv_starts[sender]
    inputs = recv_in[gather_rows]
    grad_rows = recv_grad[gather_rows]
    gate_weight_grad, up_weight_grad, down_grad, input_rows = expert_backward(
        inputs, grad_rows, w_gate[0], w_up[0], w_down[0]
    )
    back_slot = jnp.arange(experts * capacity, dtype=jnp.int32)
    back_off = back_slot % capacity
    back_sender = back_slot // capacity
    kept = back_off < recv_counts[back_sender]
    back_pos = jnp.minimum(recv_starts[back_sender] + back_off, assigned - 1)
    returned = jnp.where(kept[:, None], input_rows[back_pos], 0)
    arrived = lax.all_to_all(
        returned.reshape(experts, capacity, model_width),
        ("group", "expert"),
        split_axis=0,
        concat_axis=0,
        tiled=True,
    )
    arrived = arrived.reshape(experts * capacity, model_width)
    summed = contract_rows(slot_select, arrived)
    grad_in = summed.astype(jnp.bfloat16)
    return (grad_in, gate_weight_grad[None], up_weight_grad[None], down_grad[None])


def hop(value, axis, mask):
    size = lax.axis_size(axis)
    return lax.ppermute(value, axis, [(i, i ^ mask) for i in range(size)])


def after(value, *earlier):
    return lax.optimization_barrier((value, *earlier))[0]


def divisor(extent, limit):
    return next(w for w in range(limit, 0, -128) if extent % w == 0)


def slot_kernel(bounds, place, weight, *rest, sizes, first, last):
    near, far, (wg_hbm, wu_hbm, wd_hbm) = rest[:5], rest[5:10], rest[10:13]
    rest = rest[13:] if first else rest[18:]
    (x_out, g_out, h_out, gg_out, ug_out, near_sum, far_sum) = rest[:7]
    (toks, wg, wu, wd, pick, xt, gt, ht, ggt, ugt, spread, in_sem, out_sem) = rest[7:]
    model_width, hidden_width = wg.shape
    wide, slim = divisor(model_width, 512), divisor(hidden_width, 256)
    offset, count = bounds[0], bounds[1]
    tokens = near[0].shape[1]
    half = 4 * tokens
    sources = []
    for kind in range(2):
        for side, pieces in enumerate((near, far)):
            passed = pieces[3 + kind]
            parts = [p.at[kind] for p in pieces[:3]] + [passed.at[passed.shape[0] - 1]]
            for i, part in enumerate(parts):
                sources.append((part, toks.at[kind, pl.ds(side * half + i * tokens, tokens)]))
    sources += [(wd_hbm, wd), (wg_hbm, wg), (wu_hbm, wu)]
    loads = [pltpu.make_async_copy(s, d, in_sem.at[i]) for i, (s, d) in enumerate(sources)]
    for load in loads:
        load.start()

    def work(size):
        bf16, f32 = jnp.bfloat16, jnp.float32
        live = pl.ds(0, size)
        rows = lax.broadcasted_iota(jnp.int32, (size, 2 * half), 0)
        hit = place[...] == rows
        pick[live] = hit.astype(bf16)
        scale = jnp.sum(jnp.where(hit, weight[...], 0.0), axis=1, keepdims=True)

        def span(j, width):
            return pl.ds(pl.multiple_of(j * width, width), width)

        def take(source, into, factor):
            def step(j, c):
                cols = span(j, wide)
                found = jnp.dot(pick[live], toks[source, :, cols], preferred_element_type=f32)
                into[live, cols] = (found if factor is None else factor * found).astype(bf16)
                return c

            lax.fori_loop(0, model_width // wide, step, 0)

        for load in loads[:8]:
            load.wait()
        take(0, xt, None)
        for load in loads[8:16]:
            load.wait()
        take(1, gt, scale)
        for load in loads[16:]:
            load.wait()

        def forward(j, c):
            cols = span(j, slim)
            hidden_grad = contract_cols(gt[live], wd[cols, :])
            gate_pre = jnp.dot(xt[live], wg[:, cols], preferred_element_type=f32)
            up_pre = jnp.dot(xt[live], wu[:, cols], preferred_element_type=f32)
            sigma = 1.0 / (1.0 + jnp.exp(-gate_pre))
            activated = gate_pre * sigma
            ugt[live, cols] = (hidden_grad * activated).astype(bf16)
            ht[live, cols] = (activated * up_pre).astype(bf16)
            ggt[live, cols] = (
                hidden_grad * up_pre * sigma * (1.0 + gate_pre * (1.0 - sigma))
            ).astype(bf16)
            return c

        lax.fori_loop(0, hidden_width // slim, forward, 0)
        row0 = pl.multiple_of(offset, ALIGN)
        stores = [
            pltpu.make_async_copy(src.at[live], dst.at[pl.ds(row0, size)], out_sem.at[n])
            for n, (src, dst) in enumerate(
                [(xt, x_out), (gt, g_out), (ht, h_out), (ggt, gg_out), (ugt, ug_out)]
            )
        ]
        for store in stores:
            store.start()

        def back(j, c):
            cols = span(j, wide)
            found = contract_cols(ggt[live], wg[cols, :]) + contract_cols(ugt[live], wu[cols, :])
            part = contract_rows(pick[live], found.astype(bf16)).astype(bf16)
            spread[0, :, cols] = part[half:]
            spread[1, :, cols] = part[:half]
            return c

        lax.fori_loop(0, model_width // wide, back, 0)
        for n, out in enumerate((far_sum, near_sum)):
            store = pltpu.make_async_copy(spread.at[n], out, out_sem.at[5 + n])
            store.start()
            stores.append(store)
        for store in stores:
            store.wait()
        if last:
            end = pl.ds(0, last)
            stores = []
            for n, (src, dst) in enumerate(
                [(xt, x_out), (gt, g_out), (ht, h_out), (ggt, gg_out), (ugt, ug_out)]
            ):
                src[end] = jnp.zeros((last, src.shape[1]), bf16)
                into = dst.at[pl.ds(pl.multiple_of(row0 + size, ALIGN), last)]
                stores.append(pltpu.make_async_copy(src.at[end], into, out_sem.at[n]))
                stores[-1].start()
            for store in stores:
                store.wait()

    low = -1
    for size in sizes:
        pl.when((count > low) & (count <= size))(functools.partial(work, size))
        low = size


def slot_call(bounds, place, weight, near, far, weights, kept, kept_shapes, sizes, last):
    wg, wu, wd = weights
    model_width, hidden_width = wg.shape
    half = 4 * near[0].shape[1]
    bf16 = jnp.bfloat16
    anyspace = pl.BlockSpec(memory_space=pl.ANY)
    vmem = pl.BlockSpec(memory_space=pltpu.VMEM)
    smem = pl.BlockSpec(memory_space=pltpu.SMEM)
    flops = 2 * sizes[0] * model_width * (5 * hidden_width + 6 * half)
    return pl.pallas_call(
        functools.partial(slot_kernel, sizes=sizes, first=not kept, last=last),
        out_shape=[jax.ShapeDtypeStruct(shape, bf16) for shape in kept_shapes]
        + [jax.ShapeDtypeStruct((half, model_width), bf16)] * 2,
        in_specs=[smem, vmem, vmem] + [anyspace] * (13 + len(kept)),
        out_specs=[anyspace] * 7,
        input_output_aliases={16 + n: n for n in range(len(kept))},
        scratch_shapes=[
            pltpu.VMEM((2, 2 * half, model_width), bf16),
            pltpu.VMEM((model_width, hidden_width), bf16),
            pltpu.VMEM((model_width, hidden_width), bf16),
            pltpu.VMEM((hidden_width, model_width), bf16),
            pltpu.VMEM((sizes[-1], 2 * half), bf16),
            pltpu.VMEM((sizes[-1], model_width), bf16),
            pltpu.VMEM((sizes[-1], model_width), bf16),
            pltpu.VMEM((sizes[-1], hidden_width), bf16),
            pltpu.VMEM((sizes[-1], hidden_width), bf16),
            pltpu.VMEM((sizes[-1], hidden_width), bf16),
            pltpu.VMEM((2, half, model_width), bf16),
            pltpu.SemaphoreType.DMA((19,)),
            pltpu.SemaphoreType.DMA((7,)),
        ],
        compiler_params=pltpu.CompilerParams(vmem_limit_bytes=48 * 2**20),
        cost_estimate=pl.CostEstimate(
            flops=flops, bytes_accessed=24 * 2**20, transcendentals=sizes[0] * hidden_width
        ),
    )(bounds, place, weight, *near, *far, wg, wu, wd, *kept)


def assemble(block, by_x, by_y):
    if not by_x:
        return block, block
    return jnp.concatenate([block, by_y[-1][1:2]]), jnp.concatenate([block, by_x[-1][0:1]])


def flip_to_relative(value, axis, axis_name):
    me, size = lax.axis_index(axis_name), value.shape[axis]
    bit = 1
    while bit < size:
        shape = value.shape
        split = shape[:axis] + (size // (2 * bit), 2, bit) + shape[axis + 1 :]
        whole = value.reshape(split)
        value = jnp.where((me & bit) != 0, jnp.flip(whole, axis + 1), whole).reshape(shape)
        bit *= 2
    return value


def gathered(tokens_in, out_grad, expert_ids, gate_weights, w_gate, w_up, w_down):
    groups = lax.axis_size("group")
    owners = lax.axis_size("expert")
    experts = groups * owners
    token_count, top_count = expert_ids.shape
    model_width = tokens_in.shape[1]
    hidden_width = w_gate.shape[2]
    assigned = token_count * top_count
    chips = groups // 2
    half = chips * token_count
    bf16, f32 = jnp.bfloat16, jnp.float32
    weights = (w_gate[0], w_up[0], w_down[0])

    own = jnp.stack([tokens_in, out_grad])
    my_owner = lax.axis_index("expert")

    mean = assigned // owners
    sizes = (mean, mean + mean // 2, 2 * mean)
    used_rows = assigned + owners * ALIGN
    kept_rows = used_rows + 2 * mean + owners * ALIGN
    kept_shapes = [(kept_rows, w) for w in (model_width,) * 2 + (hidden_width,) * 3]
    kept = []

    slots, ups, downs = [own], [own], [own]

    def carry():
        step = len(ups)
        rising = [(i, i + 1) for i in range(step - 1, owners - 1)]
        falling = [(i + 1, i) for i in range(owners - step)]
        if step > owners - step:
            value = jnp.where(my_owner >= step - 1, ups[-1], downs[-1])
            ups.append(lax.ppermute(value, "expert", rising + falling))
            downs.append(ups[-1])
        else:
            ups.append(lax.ppermute(ups[-1], "expert", rising))
            downs.append(lax.ppermute(downs[-1], "expert", falling))

    def settle():
        slot, value = len(slots), None
        for i in range(owners):
            gap = (i ^ slot) - i
            found = downs[gap] if gap > 0 else ups[-gap]
            value = found if value is None else jnp.where(my_owner == i, found, value)
        slots.append(value)

    def routing(came):
        came = came.reshape(groups, owners, token_count)
        came = flip_to_relative(flip_to_relative(came, 0, "group"), 1, "expert")
        came = came.reshape(chips, 2, owners, token_count).transpose(2, 1, 0, 3)
        weight = came.reshape(owners, 2 * half)
        mask = weight >= 0.0
        ones = mask.astype(jnp.int32)
        place = jnp.where(mask, jnp.cumsum(ones, axis=1) - 1, -1).reshape(owners, 1, 2 * half)
        counts = jnp.sum(ones, axis=1)
        ends = jnp.cumsum((counts + ALIGN - 1) // ALIGN * ALIGN)
        bounds = jnp.stack([jnp.concatenate([jnp.zeros((1,), jnp.int32), ends[:-1]]), counts], axis=1)
        return bounds, place, weight.reshape(owners, 1, 2 * half)

    hw = model_width // 2
    lo, hi = slice(0, hw), slice(hw, model_width)

    def total(slot, chip, cols):
        near_sum, far_sums = paired[slot]
        rows = slice(chip * token_count, (chip + 1) * token_count)
        whose = [c for c, count in enumerate(v.shape[0] // token_count for v in far_sums) for _ in range(count)]
        which = whose[chip]
        first = (chip - whose.index(which)) * token_count
        came = far_sums[which][first : first + token_count, cols]
        return near_sum[rows, cols].astype(f32) + came.astype(f32)

    def first_half(slot):
        for_x = jnp.concatenate([total(slot, 1, lo), total(slot, 3, lo)], axis=1)
        for_y = jnp.concatenate([total(slot, 2, hi), total(slot, 3, hi)], axis=1)
        return for_x.astype(bf16), for_y.astype(bf16)

    def second_half(slots_):
        for_x = [total(k, 1, hi) + started[1][k, :, hw:].astype(f32) for k in slots_]
        for_y = [total(k, 2, lo) + started[0][k, :, hw:].astype(f32) for k in slots_]
        return tuple(
            jnp.stack([jnp.concatenate(v[n : n + 2], axis=1) for n in range(0, len(v), 2)]).astype(bf16)
            for v in (for_x, for_y)
        )

    def both(for_x, for_y):
        return hop(for_x, "group", 2), hop(for_y, "group", 4)

    columns = jnp.arange(experts, dtype=jnp.int32)
    named = expert_ids[None, :, :] == columns[:, None, None]
    sent = jnp.sum(jnp.where(named, gate_weights[None], 0.0), axis=2)
    sent = jnp.where(jnp.any(named, axis=2), sent, -1.0)
    by_x, by_y, near, far = [], [], [], []
    paired, started, back = {}, (), {}
    early, late = list(range(owners - 2)), owners - 2
    route, grads = None, []
    for stage in range(owners + 3):
        new = {}
        if stage < owners:
            pair = assemble(slots[stage], by_x, by_y)
            new["cross"] = both(*pair)
            if 0 < stage < owners - 1:
                ups[-1], downs[-1] = after((ups[-1], downs[-1]), *pair)
        elif stage == owners:
            starts = [first_half(k) for k in early] + [(by_y[-1][1], by_x[-1][0])]
            new["cross"] = both(*[jnp.stack(v) for v in zip(*starts)])
        if stage < owners - 1:
            carry()
            settle()
        if stage > owners:
            slot = stage - 3
            if stage == owners + 2:
                near_sum, (far_own, far_rest) = paired[slot]
                far_rest = hop(far_rest, "group", 1)
                paired[slot] = (near_sum, (far_own, far_rest))
            sends = tuple(total(slot, chip, slice(None)).astype(bf16)[None] for chip in (1, 2))
            if slot == late:
                sends = tuple(jnp.concatenate(v) for v in zip(sends, second_half(early)))
            sends += (total(slot, 3, slice(None)).astype(bf16),)
            new["straight"] = both(*sends[:2])
            new["corner"] = hop(sends[2], "group", 6)
            if stage == owners + 2:
                far_own = hop(after(far_own, *sends), "group", 1)
                paired[slot] = (near_sum, (far_own, far_rest))
                going, rows = after(({k: back[k] for k in early if k}, kept), far_own)
                going[late] = after(back[late], far_rest)
                new["home"] = {k: hop(going[k].astype(bf16), "expert", k) for k in going}
                rows = [k[:used_rows] for k in rows]
                grads = [contract_rows(rows[0], rows[n]).astype(bf16) for n in (3, 4)]
        if 1 <= stage <= owners:
            mine = near[stage - 1]
            if stage == 1:
                mine = after(mine, ups[-1], downs[-1])
            new["far"] = tuple(hop(v, "group", 1) for v in mine)
        elif stage == owners + 1:
            near[owners] = tuple(v[-1:] for v in after(near[owners], *sends))
            new["far"] = tuple(hop(v, "group", 1) for v in near[owners])
        if stage == 0:
            route = lax.all_to_all(sent, AXES, split_axis=0, concat_axis=0, tiled=True)
        if stage == 1:
            route = routing(after(route, ups[-1], downs[-1]))
        if 2 <= stage < owners + 2:
            slot = stage - 2
            bounds, place, weight = route
            far.append(new.pop("far"))
            pieces = [list(v[slot]) + [v[slot + 1][-1], v[slot + 1][-2]] for v in (near, far)]
            final = owners * ALIGN if slot == owners - 1 else 0
            *kept, near_sum, far_sum = slot_call(
                bounds[slot], place[slot], weight[slot], *pieces, weights, kept, kept_shapes, sizes, final
            )
            cut = far_sum.shape[0] // 2 if slot < owners - 1 else token_count
            far_sums = (far_sum[:cut], far_sum[cut:])
            if slot < owners - 1:
                far_sums = tuple(hop(v, "group", 1) for v in far_sums)
            new["paired"] = (near_sum, far_sums)
        arrays = (new, ups, downs, slots, near, far, paired, started, back, kept, route, grads, by_x, by_y)
        new, ups, downs, slots, near, far, paired, started, back, kept, route, grads, by_x, by_y = (
            lax.optimization_barrier(arrays)
        )
        if "cross" in new:
            x, y = new["cross"]
            if stage < owners:
                by_x.append(x)
                by_y.append(y)
                near.append((slots[stage], x, y))
            else:
                near.append((x, y))
                started = (x, y)
        if "far" in new:
            far.append(new["far"])
        if "paired" in new:
            paired[stage - 2] = new["paired"]
        if "straight" in new:
            slot = stage - 3
            x, y = [v.astype(f32) for v in new["straight"]]
            back[slot] = total(slot, 0, slice(None)) + new["corner"].astype(f32)
            back[slot] += x[0] + y[0]
            if slot == late:
                for k in early:
                    half = slice(k % 2 * hw, (k % 2 + 1) * hw)
                    left = total(k, 0, lo) + started[0][k, :, :hw].astype(f32) + y[1 + k // 2][:, half]
                    right = total(k, 0, hi) + started[1][k, :, :hw].astype(f32) + x[1 + k // 2][:, half]
                    back[k] = jnp.concatenate([left, right], axis=1)
        if "home" in new:
            back.update(new["home"])
    last = owners - 1
    back[last] = hop(back[last].astype(bf16), "expert", last)
    grad_in = sum(back[slot].astype(f32) for slot in range(owners)).astype(bf16)

    hidden, grad_rows = kept[2][:used_rows], kept[1][:used_rows]
    gate_weight_grad, up_weight_grad = grads
    down_grad = contract_rows(hidden, grad_rows).astype(bf16)
    return (grad_in, gate_weight_grad[None], up_weight_grad[None], down_grad[None])


def body(*args):
    groups, owners = lax.axis_size("group"), lax.axis_size("expert")
    token_count, top_count = args[2].shape
    spread = groups * owners * token_count <= 4 * token_count * top_count
    square = groups.bit_count() == 1 and len(bin(groups)) == len("0b1000")
    line = owners > 2 and owners.bit_count() == 1
    return (gathered if spread and square and line else routed)(*args)


def solution(mesh):
    rows = P(AXES, None)
    mats = P(AXES, None, None)
    return jax.shard_map(
        body,
        mesh=mesh,
        in_specs=(rows, rows, rows, rows, mats, mats, mats),
        out_specs=(rows, mats, mats, mats),
        check_vma=False,
    )
```

```python
import functools

import jax
import jax.numpy as jnp
from jax import lax
from jax.experimental import pallas as pl
from jax.experimental.pallas import tpu as pltpu
from jax.sharding import PartitionSpec as P

AXES = ("group", "expert")
ALIGN = 16


def contract_rows(first_op, second_op):
    return lax.dot_general(
        first_op, second_op, (((0,), (0,)), ((), ())), preferred_element_type=jnp.float32
    )


def contract_cols(first_op, second_op):
    return lax.dot_general(
        first_op, second_op, (((1,), (1,)), ((), ())), preferred_element_type=jnp.float32
    )


def expert_backward(inputs, grad_rows, gate_mat, up_mat, down_mat):
    gate_pre = jnp.dot(inputs, gate_mat, preferred_element_type=jnp.float32)
    up_pre = jnp.dot(inputs, up_mat, preferred_element_type=jnp.float32)
    sigma_gate = jax.nn.sigmoid(gate_pre)
    activated = gate_pre * sigma_gate
    hidden = (activated * up_pre).astype(jnp.bfloat16)
    hidden_grad = contract_cols(grad_rows, down_mat)
    down_grad = contract_rows(hidden, grad_rows).astype(jnp.bfloat16)
    gate_grad_rows = (
        hidden_grad * up_pre * sigma_gate * (1.0 + gate_pre * (1.0 - sigma_gate))
    ).astype(jnp.bfloat16)
    up_grad_rows = (hidden_grad * activated).astype(jnp.bfloat16)
    input_rows = (
        contract_cols(gate_grad_rows, gate_mat) + contract_cols(up_grad_rows, up_mat)
    ).astype(jnp.bfloat16)
    gate_weight_grad = contract_rows(inputs, gate_grad_rows).astype(jnp.bfloat16)
    up_weight_grad = contract_rows(inputs, up_grad_rows).astype(jnp.bfloat16)
    return (gate_weight_grad, up_weight_grad, down_grad, input_rows)


def routed(tokens_in, out_grad, expert_ids, gate_weights, w_gate, w_up, w_down):
    groups = lax.axis_size("group")
    owners = lax.axis_size("expert")
    experts = groups * owners
    token_count, top_count = expert_ids.shape
    model_width = tokens_in.shape[1]
    assigned = token_count * top_count
    capacity = 2 * assigned // experts
    flat_ids = expert_ids.reshape(assigned)
    columns = jnp.arange(experts, dtype=jnp.int32)
    counts = jnp.sum((flat_ids[:, None] == columns[None, :]).astype(jnp.int32), axis=0)
    starts = jnp.cumsum(counts) - counts
    sorted_rows = jnp.argsort(flat_ids, stable=True)
    gate_flat = gate_weights.reshape(assigned)
    sender_pos = jnp.arange(experts, dtype=jnp.int32)
    token_cols = jnp.arange(token_count, dtype=jnp.int32)
    slot_pos = jnp.arange(experts * capacity, dtype=jnp.int32)
    slot_owner = slot_pos // capacity
    slot_index = slot_pos % capacity
    filled = slot_index < counts[slot_owner]
    source = sorted_rows[jnp.minimum(starts[slot_owner] + slot_index, assigned - 1)]
    slot_token = jnp.where(filled, source // top_count, -1)
    slot_select = (slot_token[:, None] == token_cols[None, :]).astype(jnp.bfloat16)
    rows_in = jnp.dot(slot_select, tokens_in, preferred_element_type=jnp.float32).astype(
        jnp.bfloat16
    )
    picked_grad = jnp.dot(slot_select, out_grad, preferred_element_type=jnp.float32)
    rows_grad = (gate_flat[source][:, None] * picked_grad).astype(jnp.bfloat16)
    recv_in, recv_grad, recv_counts = (
        lax.all_to_all(
            rows_in.reshape(experts, capacity, model_width),
            ("group", "expert"),
            split_axis=0,
            concat_axis=0,
            tiled=True,
        ),
        lax.all_to_all(
            rows_grad.reshape(experts, capacity, model_width),
            ("group", "expert"),
            split_axis=0,
            concat_axis=0,
            tiled=True,
        ),
        lax.all_to_all(counts, ("group", "expert"), split_axis=0, concat_axis=0, tiled=True),
    )
    sender_base = sender_pos * capacity
    recv_in = recv_in.reshape(experts * capacity, model_width)
    recv_grad = recv_grad.reshape(experts * capacity, model_width)
    recv_ends = jnp.cumsum(recv_counts)
    recv_starts = recv_ends - recv_counts
    live_rows = jnp.arange(assigned, dtype=jnp.int32)
    sender = jnp.minimum(
        jnp.sum((live_rows[:, None] >= recv_ends[None, :]).astype(jnp.int32), axis=1), experts - 1
    )
    gather_rows = sender_base[sender] + live_rows - recv_starts[sender]
    inputs = recv_in[gather_rows]
    grad_rows = recv_grad[gather_rows]
    gate_weight_grad, up_weight_grad, down_grad, input_rows = expert_backward(
        inputs, grad_rows, w_gate[0], w_up[0], w_down[0]
    )
    back_slot = jnp.arange(experts * capacity, dtype=jnp.int32)
    back_off = back_slot % capacity
    back_sender = back_slot // capacity
    kept = back_off < recv_counts[back_sender]
    back_pos = jnp.minimum(recv_starts[back_sender] + back_off, assigned - 1)
    returned = jnp.where(kept[:, None], input_rows[back_pos], 0)
    arrived = lax.all_to_all(
        returned.reshape(experts, capacity, model_width),
        ("group", "expert"),
        split_axis=0,
        concat_axis=0,
        tiled=True,
    )
    arrived = arrived.reshape(experts * capacity, model_width)
    summed = contract_rows(slot_select, arrived)
    grad_in = summed.astype(jnp.bfloat16)
    return (grad_in, gate_weight_grad[None], up_weight_grad[None], down_grad[None])


def hop(value, axis, mask):
    size = lax.axis_size(axis)
    return lax.ppermute(value, axis, [(i, i ^ mask) for i in range(size)])


def after(value, *earlier):
    return lax.optimization_barrier((value, *earlier))[0]


def divisor(extent, limit):
    return next(w for w in range(limit, 0, -128) if extent % w == 0)


def slot_kernel(bounds, place, weight, *rest, sizes, first, last):
    near, far, (wg_hbm, wu_hbm, wd_hbm) = rest[:5], rest[5:10], rest[10:13]
    rest = rest[13:] if first else rest[18:]
    (x_out, g_out, h_out, gg_out, ug_out, near_sum, far_sum) = rest[:7]
    (toks, wg, wu, wd, pick, xt, gt, ht, ggt, ugt, spread, in_sem, out_sem) = rest[7:]
    model_width, hidden_width = wg.shape
    wide, slim = divisor(model_width, 512), divisor(hidden_width, 256)
    offset, count = bounds[0], bounds[1]
    tokens = near[0].shape[1]
    half = 4 * tokens
    sources = []
    for kind in range(2):
        for side, pieces in enumerate((near, far)):
            passed = pieces[3 + kind]
            parts = [p.at[kind] for p in pieces[:3]] + [passed.at[passed.shape[0] - 1]]
            for i, part in enumerate(parts):
                sources.append((part, toks.at[kind, pl.ds(side * half + i * tokens, tokens)]))
    sources += [(wd_hbm, wd), (wg_hbm, wg), (wu_hbm, wu)]
    loads = [pltpu.make_async_copy(s, d, in_sem.at[i]) for i, (s, d) in enumerate(sources)]
    for load in loads:
        load.start()

    def work(size):
        bf16, f32 = jnp.bfloat16, jnp.float32
        live = pl.ds(0, size)
        rows = lax.broadcasted_iota(jnp.int32, (size, 2 * half), 0)
        hit = place[...] == rows
        pick[live] = hit.astype(bf16)
        scale = jnp.sum(jnp.where(hit, weight[...], 0.0), axis=1, keepdims=True)

        def span(j, width):
            return pl.ds(pl.multiple_of(j * width, width), width)

        def take(source, into, factor):
            def step(j, c):
                cols = span(j, wide)
                found = jnp.dot(pick[live], toks[source, :, cols], preferred_element_type=f32)
                into[live, cols] = (found if factor is None else factor * found).astype(bf16)
                return c

            lax.fori_loop(0, model_width // wide, step, 0)

        for load in loads[:8]:
            load.wait()
        take(0, xt, None)
        for load in loads[8:16]:
            load.wait()
        take(1, gt, scale)
        for load in loads[16:]:
            load.wait()

        def forward(j, c):
            cols = span(j, slim)
            hidden_grad = contract_cols(gt[live], wd[cols, :])
            gate_pre = jnp.dot(xt[live], wg[:, cols], preferred_element_type=f32)
            up_pre = jnp.dot(xt[live], wu[:, cols], preferred_element_type=f32)
            sigma = 1.0 / (1.0 + jnp.exp(-gate_pre))
            activated = gate_pre * sigma
            ugt[live, cols] = (hidden_grad * activated).astype(bf16)
            ht[live, cols] = (activated * up_pre).astype(bf16)
            ggt[live, cols] = (
                hidden_grad * up_pre * sigma * (1.0 + gate_pre * (1.0 - sigma))
            ).astype(bf16)
            return c

        lax.fori_loop(0, hidden_width // slim, forward, 0)
        row0 = pl.multiple_of(offset, ALIGN)
        stores = [
            pltpu.make_async_copy(src.at[live], dst.at[pl.ds(row0, size)], out_sem.at[n])
            for n, (src, dst) in enumerate(
                [(xt, x_out), (gt, g_out), (ht, h_out), (ggt, gg_out), (ugt, ug_out)]
            )
        ]
        for store in stores:
            store.start()

        def back(j, c):
            cols = span(j, wide)
            found = contract_cols(ggt[live], wg[cols, :]) + contract_cols(ugt[live], wu[cols, :])
            part = contract_rows(pick[live], found.astype(bf16)).astype(bf16)
            spread[0, :, cols] = part[half:]
            spread[1, :, cols] = part[:half]
            return c

        lax.fori_loop(0, model_width // wide, back, 0)
        for n, out in enumerate((far_sum, near_sum)):
            store = pltpu.make_async_copy(spread.at[n], out, out_sem.at[5 + n])
            store.start()
            stores.append(store)
        for store in stores:
            store.wait()
        if last:
            end = pl.ds(0, last)
            stores = []
            for n, (src, dst) in enumerate(
                [(xt, x_out), (gt, g_out), (ht, h_out), (ggt, gg_out), (ugt, ug_out)]
            ):
                src[end] = jnp.zeros((last, src.shape[1]), bf16)
                into = dst.at[pl.ds(pl.multiple_of(row0 + size, ALIGN), last)]
                stores.append(pltpu.make_async_copy(src.at[end], into, out_sem.at[n]))
                stores[-1].start()
            for store in stores:
                store.wait()

    low = -1
    for size in sizes:
        fits = (count <= size) | (size == sizes[-1])
        pl.when((count > low) & fits)(functools.partial(work, size))
        low = size


def slot_call(bounds, place, weight, near, far, weights, kept, kept_shapes, sizes, last):
    wg, wu, wd = weights
    model_width, hidden_width = wg.shape
    half = 4 * near[0].shape[1]
    bf16 = jnp.bfloat16
    anyspace = pl.BlockSpec(memory_space=pl.ANY)
    vmem = pl.BlockSpec(memory_space=pltpu.VMEM)
    smem = pl.BlockSpec(memory_space=pltpu.SMEM)
    flops = 2 * sizes[0] * model_width * (5 * hidden_width + 6 * half)
    return pl.pallas_call(
        functools.partial(slot_kernel, sizes=sizes, first=not kept, last=last),
        out_shape=[jax.ShapeDtypeStruct(shape, bf16) for shape in kept_shapes]
        + [jax.ShapeDtypeStruct((half, model_width), bf16)] * 2,
        in_specs=[smem, vmem, vmem] + [anyspace] * (13 + len(kept)),
        out_specs=[anyspace] * 7,
        input_output_aliases={16 + n: n for n in range(len(kept))},
        scratch_shapes=[
            pltpu.VMEM((2, 2 * half, model_width), bf16),
            pltpu.VMEM((model_width, hidden_width), bf16),
            pltpu.VMEM((model_width, hidden_width), bf16),
            pltpu.VMEM((hidden_width, model_width), bf16),
            pltpu.VMEM((sizes[-1], 2 * half), bf16),
            pltpu.VMEM((sizes[-1], model_width), bf16),
            pltpu.VMEM((sizes[-1], model_width), bf16),
            pltpu.VMEM((sizes[-1], hidden_width), bf16),
            pltpu.VMEM((sizes[-1], hidden_width), bf16),
            pltpu.VMEM((sizes[-1], hidden_width), bf16),
            pltpu.VMEM((2, half, model_width), bf16),
            pltpu.SemaphoreType.DMA((19,)),
            pltpu.SemaphoreType.DMA((7,)),
        ],
        compiler_params=pltpu.CompilerParams(vmem_limit_bytes=48 * 2**20),
        cost_estimate=pl.CostEstimate(
            flops=flops, bytes_accessed=24 * 2**20, transcendentals=sizes[0] * hidden_width
        ),
    )(bounds, place, weight, *near, *far, wg, wu, wd, *kept)


def assemble(block, by_x, by_y):
    if not by_x:
        return block, block
    return jnp.concatenate([block, by_y[-1][1:2]]), jnp.concatenate([block, by_x[-1][0:1]])


def flip_to_relative(value, axis, axis_name):
    me, size = lax.axis_index(axis_name), value.shape[axis]
    bit = 1
    while bit < size:
        shape = value.shape
        split = shape[:axis] + (size // (2 * bit), 2, bit) + shape[axis + 1 :]
        whole = value.reshape(split)
        value = jnp.where((me & bit) != 0, jnp.flip(whole, axis + 1), whole).reshape(shape)
        bit *= 2
    return value


def gathered(tokens_in, out_grad, expert_ids, gate_weights, w_gate, w_up, w_down):
    groups = lax.axis_size("group")
    owners = lax.axis_size("expert")
    experts = groups * owners
    token_count, top_count = expert_ids.shape
    model_width = tokens_in.shape[1]
    hidden_width = w_gate.shape[2]
    assigned = token_count * top_count
    chips = groups // 2
    half = chips * token_count
    bf16, f32 = jnp.bfloat16, jnp.float32
    weights = (w_gate[0], w_up[0], w_down[0])

    own = jnp.stack([tokens_in, out_grad])
    my_owner = lax.axis_index("expert")

    mean = assigned // owners
    sizes = (mean, mean + mean // 2, 2 * mean)
    used_rows = assigned + owners * ALIGN
    kept_rows = used_rows + 2 * mean + owners * ALIGN
    kept_shapes = [(kept_rows, w) for w in (model_width,) * 2 + (hidden_width,) * 3]
    kept = []

    slots, ups, downs = [own], [own], [own]

    def carry():
        step = len(ups)
        rising = [(i, i + 1) for i in range(step - 1, owners - 1)]
        falling = [(i + 1, i) for i in range(owners - step)]
        if step > owners - step:
            value = jnp.where(my_owner >= step - 1, ups[-1], downs[-1])
            ups.append(lax.ppermute(value, "expert", rising + falling))
            downs.append(ups[-1])
        else:
            ups.append(lax.ppermute(ups[-1], "expert", rising))
            downs.append(lax.ppermute(downs[-1], "expert", falling))

    def settle():
        slot, value = len(slots), None
        for i in range(owners):
            gap = (i ^ slot) - i
            found = downs[gap] if gap > 0 else ups[-gap]
            value = found if value is None else jnp.where(my_owner == i, found, value)
        slots.append(value)

    def routing(came):
        came = came.reshape(groups, owners, token_count)
        came = flip_to_relative(flip_to_relative(came, 0, "group"), 1, "expert")
        came = came.reshape(chips, 2, owners, token_count).transpose(2, 1, 0, 3)
        weight = came.reshape(owners, 2 * half)
        mask = weight >= 0.0
        ones = mask.astype(jnp.int32)
        place = jnp.where(mask, jnp.cumsum(ones, axis=1) - 1, -1).reshape(owners, 1, 2 * half)
        counts = jnp.sum(ones, axis=1)
        ends = jnp.cumsum((counts + ALIGN - 1) // ALIGN * ALIGN)
        bounds = jnp.stack([jnp.concatenate([jnp.zeros((1,), jnp.int32), ends[:-1]]), counts], axis=1)
        return bounds, place, weight.reshape(owners, 1, 2 * half)

    hw = model_width // 2
    lo, hi = slice(0, hw), slice(hw, model_width)

    def total(slot, chip, cols):
        near_sum, far_sums = paired[slot]
        rows = slice(chip * token_count, (chip + 1) * token_count)
        whose = [c for c, count in enumerate(v.shape[0] // token_count for v in far_sums) for _ in range(count)]
        which = whose[chip]
        first = (chip - whose.index(which)) * token_count
        came = far_sums[which][first : first + token_count, cols]
        return near_sum[rows, cols].astype(f32) + came.astype(f32)

    def first_half(slot):
        for_x = jnp.concatenate([total(slot, 1, lo), total(slot, 3, lo)], axis=1)
        for_y = jnp.concatenate([total(slot, 2, hi), total(slot, 3, hi)], axis=1)
        return for_x.astype(bf16), for_y.astype(bf16)

    def second_half(slots_):
        for_x = [total(k, 1, hi) + started[1][k, :, hw:].astype(f32) for k in slots_]
        for_y = [total(k, 2, lo) + started[0][k, :, hw:].astype(f32) for k in slots_]
        return tuple(
            jnp.stack([jnp.concatenate(v[n : n + 2], axis=1) for n in range(0, len(v), 2)]).astype(bf16)
            for v in (for_x, for_y)
        )

    def both(for_x, for_y):
        return hop(for_x, "group", 2), hop(for_y, "group", 4)

    columns = jnp.arange(experts, dtype=jnp.int32)
    named = expert_ids[None, :, :] == columns[:, None, None]
    sent = jnp.sum(jnp.where(named, gate_weights[None], 0.0), axis=2)
    sent = jnp.where(jnp.any(named, axis=2), sent, -1.0)
    by_x, by_y, near, far = [], [], [], []
    paired, started, back = {}, (), {}
    early, late = list(range(owners - 2)), owners - 2
    route, grads = None, []
    for stage in range(owners + 3):
        new = {}
        if stage < owners:
            pair = assemble(slots[stage], by_x, by_y)
            new["cross"] = both(*pair)
            if 0 < stage < owners - 1:
                ups[-1], downs[-1] = after((ups[-1], downs[-1]), *pair)
        elif stage == owners:
            starts = [first_half(k) for k in early] + [(by_y[-1][1], by_x[-1][0])]
            new["cross"] = both(*[jnp.stack(v) for v in zip(*starts)])
        if stage < owners - 1:
            carry()
            settle()
        if stage > owners:
            slot = stage - 3
            if stage == owners + 2:
                near_sum, (far_own, far_rest) = paired[slot]
                paired[slot] = (near_sum, (far_own, hop(far_rest, "group", 1)))
            sends = tuple(total(slot, chip, slice(None)).astype(bf16)[None] for chip in (1, 2))
            if slot == late:
                sends = tuple(jnp.concatenate(v) for v in zip(sends, second_half(early)))
            sends += (total(slot, 3, slice(None)).astype(bf16),)
            new["straight"] = both(*sends[:2])
            new["corner"] = hop(sends[2], "group", 6)
            if stage == owners + 2:
                far_own = hop(after(far_own, *sends), "group", 1)
                paired[slot] = (near_sum, (far_own, paired[slot][1][1]))
                going, rows = after(({k: back[k] for k in back if k}, kept), far_own)
                new["home"] = {k: hop(going[k].astype(bf16), "expert", k) for k in going}
                rows = [k[:used_rows] for k in rows]
                grads = [contract_rows(rows[0], rows[n]).astype(bf16) for n in (3, 4)]
        if 1 <= stage <= owners:
            mine = near[stage - 1]
            if stage == 1:
                mine = after(mine, ups[-1], downs[-1])
            new["far"] = tuple(hop(v, "group", 1) for v in mine)
        elif stage == owners + 1:
            near[owners] = tuple(v[-1:] for v in after(near[owners], *sends))
            new["far"] = tuple(hop(v, "group", 1) for v in near[owners])
        if stage == 0:
            route = lax.all_to_all(sent, AXES, split_axis=0, concat_axis=0, tiled=True)
        if stage == 1:
            route = routing(after(route, ups[-1], downs[-1]))
        if 2 <= stage < owners + 2:
            slot = stage - 2
            bounds, place, weight = route
            far.append(new.pop("far"))
            pieces = [list(v[slot]) + [v[slot + 1][-1], v[slot + 1][-2]] for v in (near, far)]
            final = owners * ALIGN if slot == owners - 1 else 0
            *kept, near_sum, far_sum = slot_call(
                bounds[slot], place[slot], weight[slot], *pieces, weights, kept, kept_shapes, sizes, final
            )
            cut = far_sum.shape[0] // 2 if slot < owners - 1 else token_count
            far_sums = (far_sum[:cut], far_sum[cut:])
            if slot < owners - 1:
                far_sums = tuple(hop(v, "group", 1) for v in far_sums)
            new["paired"] = (near_sum, far_sums)
        arrays = (new, ups, downs, slots, near, far, paired, started, back, kept, route, grads, by_x, by_y)
        new, ups, downs, slots, near, far, paired, started, back, kept, route, grads, by_x, by_y = (
            lax.optimization_barrier(arrays)
        )
        if "cross" in new:
            x, y = new["cross"]
            if stage < owners:
                by_x.append(x)
                by_y.append(y)
                near.append((slots[stage], x, y))
            else:
                near.append((x, y))
                started = (x, y)
        if "far" in new:
            far.append(new["far"])
        if "paired" in new:
            paired[stage - 2] = new["paired"]
        if "straight" in new:
            slot = stage - 3
            x, y = [v.astype(f32) for v in new["straight"]]
            back[slot] = total(slot, 0, slice(None)) + new["corner"].astype(f32)
            back[slot] += x[0] + y[0]
            if slot == late:
                for k in early:
                    half = slice(k % 2 * hw, (k % 2 + 1) * hw)
                    left = total(k, 0, lo) + started[0][k, :, :hw].astype(f32) + y[1 + k // 2][:, half]
                    right = total(k, 0, hi) + started[1][k, :, :hw].astype(f32) + x[1 + k // 2][:, half]
                    back[k] = jnp.concatenate([left, right], axis=1)
        if "home" in new:
            back.update(new["home"])
    last = owners - 1
    back[last] = hop(back[last].astype(bf16), "expert", last)
    grad_in = sum(back[slot].astype(f32) for slot in range(owners)).astype(bf16)

    hidden, grad_rows = kept[2][:used_rows], kept[1][:used_rows]
    gate_weight_grad, up_weight_grad = grads
    down_grad = contract_rows(hidden, grad_rows).astype(bf16)
    return (grad_in, gate_weight_grad[None], up_weight_grad[None], down_grad[None])


def body(*args):
    groups, owners = lax.axis_size("group"), lax.axis_size("expert")
    token_count, top_count = args[2].shape
    spread = groups * owners * token_count <= 4 * token_count * top_count
    square = groups.bit_count() == 1 and len(bin(groups)) == len("0b1000")
    line = owners > 2 and owners.bit_count() == 1
    return (gathered if spread and square and line else routed)(*args)


def solution(mesh):
    rows = P(AXES, None)
    mats = P(AXES, None, None)
    return jax.shard_map(
        body,
        mesh=mesh,
        in_specs=(rows, rows, rows, rows, mats, mats, mats),
        out_specs=(rows, mats, mats, mats),
        check_vma=False,
    )
```
